32 devices in a mesh: sky: 4 (over y, x), exp: 8 (over z, core).
Axes of the slice: x: 2, y: 2, z: 4, core: 2. Of those that a mesh axis runs over, the one named last changes fastest.
Arguments:
- obs_weight: float32 [4, 8, 8, 1024], P('sky', 'exp'), may hold values from 0.25 to 4
- magnitude: float32 [4, 8, 8, 1024], P('sky', 'exp'), may hold values from -18 to 18
- star_id: int32 [4, 8, 8, 1024], P('sky', 'exp'), may hold values from 0 to 4095
- peer_count: int32 [4, 8, 8], P('sky', 'exp'), may hold values from 1 to 1024, 6144 in all within a row
- zp_index: int32 [4, 8, 8, 1024], P('sky', 'exp'), may hold values from 0 to 12095
Outputs:
- zero_points: float32 [96768], P('exp')
- residual: float32 [96768], P('exp')
The draws below stay inside these ranges and needn't reach their ends.
Inputs may be any that keep to these rules, and one draw needn't show every extreme that they name: `peer_count`: each device's counts over the 8 owners sum to 6144, and one of them equals 1024.
All inputs are finite; a program needn't handle non-finite values.
Results may differ from the reference program's by a relative error of at most 0.0003.
Values sent between devices are 32-bit elements; how exact they have to be, the bound alone decides.
No kernel may reach another device: no remote copies, remote signals or barrier semaphores. Data moves between devices by JAX's collectives and lax.ppermute only.
A program may use at most 64 MiB of HBM per device.

```python
import math
import jax
import jax.numpy as jnp
import numpy as np

CAP = 1024
STAR_DEV = 4096
ITERS = 2
ZP_DEV = 12096
N_SKY = 4
N_EXP = 8


def touch_ends(array, rng, smallest, high):
    longest = array.shape.index(max(array.shape))
    spots = []
    for shift in (0, 1):
        where = [jax.random.randint(jax.random.fold_in(rng, axis), (), 0, length) for axis, length in enumerate(array.shape)]
        where[longest] = (where[longest] + shift) % array.shape[longest]
        spots.append(tuple(where))
    return array.at[spots[0]].set(smallest).at[spots[1]].set(high)


def level_of(stream_key, dims, pieces, least, largest):
    def one(position, shards_of):
        steps = jax.random.uniform(jax.random.fold_in(jax.random.fold_in(stream_key, 6), position), (shards_of,), jnp.float32, least / len(pieces), largest / len(pieces))
        return jnp.repeat(jnp.exp(steps), dims[position] // shards_of).reshape((-1,) + (1,) * (len(dims) - position - 1))

    level = one(*pieces[0])
    for cut in pieces[1:]:
        level = level * one(*cut)
    return level


def profile(amount, total, limit, slope):
    loads = [(1 << 20) // math.isqrt(standing ** slope) + 1 for standing in range(2, amount + 1)]
    surplus, holding = total - limit - (amount - 1), [1] * (amount - 1)
    while surplus > 0:
        candidates = [i for i in range(amount - 1) if holding[i] < limit]
        mass, remaining = sum([loads[i] for i in candidates]), surplus
        for i in candidates:
            extra = min(limit - holding[i], max(1, remaining * loads[i] // mass), surplus)
            holding[i] = holding[i] + extra
            surplus = surplus - extra
    return np.array([limit] + holding)


def uneven_parts(stream_key, number_of, total, reach, lean):
    if number_of == 2:
        one = jax.random.randint(stream_key, (), max(1, total - reach), min(reach, total - 1) + 1)
        return jnp.stack([one, total - one])
    tallies = jnp.asarray(profile(number_of, total, reach, lean), jnp.int32)
    couples = (number_of - 1) // 2
    donor, taker = tallies[1:1 + 2 * couples:2], tallies[2:2 + 2 * couples:2]
    slack = jnp.minimum(donor - 1, reach - taker)
    shifted = jax.random.randint(jax.random.fold_in(stream_key, 1), (couples,), 0, 1 << 20) % (slack + 1)
    tallies = tallies.at[1:1 + 2 * couples:2].set(donor - shifted).at[2:2 + 2 * couples:2].set(taker + shifted)
    return tallies[jax.random.permutation(jax.random.fold_in(stream_key, 2), number_of)]


def noise(key, extent, deviation, most, cuts=(), held_as=jnp.bfloat16):
    result = deviation * jax.random.normal(key, extent, jnp.float32)
    if cuts:
        result = result * level_of(key, extent, cuts, -0.22, 0.18)
    return jnp.clip(result, -most, most).astype(held_as)


def setup_inputs(seed: int = 0) -> dict:
    seeds = jax.random.split(jax.random.key(seed), 6)
    obs_weight = jnp.clip(jnp.exp(math.log(4.0) - 2.7725887 * jax.random.uniform(seeds[0], (N_SKY, N_EXP, N_EXP, CAP), jnp.float32) ** level_of(seeds[0], (N_SKY, N_EXP, N_EXP, CAP), ((0, 4), (1, 8)), -0.2, 0.2)), 0.25, 4.0)
    magnitude = noise(seeds[1], (N_SKY, N_EXP, N_EXP, CAP), 3.0, 18.0, ((0, 4), (1, 8)), jnp.float32)
    star_id = touch_ends(jax.random.randint(seeds[2], (N_SKY, N_EXP, N_EXP, CAP), 0, STAR_DEV), jax.random.fold_in(seeds[2], 1), 0, STAR_DEV - 1).astype(jnp.int32)
    peer_count = jax.vmap(lambda own: uneven_parts(own, N_EXP, N_EXP * CAP * 3 // 4, CAP, 2))(jax.random.split(seeds[3], N_SKY * N_EXP)).reshape((N_SKY, N_EXP, N_EXP)).astype(jnp.int32)
    zp_index = touch_ends(jax.random.randint(seeds[4], (N_SKY, N_EXP, N_EXP, CAP), 0, ZP_DEV), jax.random.fold_in(seeds[4], 1), 0, ZP_DEV - 1).astype(jnp.int32)
    return dict(obs_weight=obs_weight, magnitude=magnitude, star_id=star_id, peer_count=peer_count, zp_index=zp_index)


ridge = 1.0
prior = 1.0


def reference(obs_weight, magnitude, star_id, peer_count, zp_index):
    n_sky = obs_weight.shape[0]
    n_exp = obs_weight.shape[1]
    slots = jnp.arange(CAP, dtype=jnp.int32)
    live = (slots[None, None, None, :] < peer_count[..., None]).astype(jnp.float32)
    weight = obs_weight * live
    device = (jnp.arange(n_sky, dtype=jnp.int32)[:, None] * n_exp + jnp.arange(n_exp, dtype=jnp.int32)[None, :])
    segment = (device[:, :, None, None] * STAR_DEV + star_id).reshape(-1)
    nstars = n_sky * n_exp * STAR_DEV
    wsum = prior + jax.ops.segment_sum(weight.reshape(-1), segment, nstars)
    owner = jnp.arange(n_exp, dtype=jnp.int32)[None, None, :, None]
    target = (owner * ZP_DEV + jnp.transpose(zp_index, (0, 2, 1, 3))).reshape(-1)
    flat_w = weight.reshape(-1)

    def reduce_slots(values):
        flat = values.reshape(-1)
        mean = jax.ops.segment_sum(flat_w * flat, segment, nstars) / wsum
        term = flat_w * (flat - mean[segment])
        return jax.ops.segment_sum(term, target, n_exp * ZP_DEV)

    def operate(field):
        return reduce_slots(field[target]) + ridge * field

    right = reduce_slots(magnitude)
    zero_points = jnp.zeros_like(right)
    residual = right
    direction = right
    norm_now = jnp.sum(residual * residual)
    for step in range(ITERS):
        image = operate(direction)
        alpha = norm_now / jnp.sum(direction * image)
        zero_points = zero_points + alpha * direction
        residual = residual - alpha * image
        norm_next = jnp.sum(residual * residual)
        direction = residual + (norm_next / norm_now) * direction
        norm_now = norm_next
    return zero_points, residual
```

```python
import functools

import jax
import jax.numpy as jnp
from jax import lax
from jax.experimental import pallas as pl
from jax.experimental.pallas import tpu as pltpu
from jax.sharding import PartitionSpec as P

STAR_DEV = 4096
ZP_DEV = 12096
LANES = 128
SUB = 8
ridge = 1.0
prior = 1.0

f32 = jnp.float32
bf16 = jnp.bfloat16
i16 = jnp.int16
STAR_ROWS = STAR_DEV // LANES
ZP_ROWS = -(-ZP_DEV // (LANES * 16)) * 16
CONTRACT_LANES = (((1,), (1,)), ((), ()))


def hot_rows(index, values, rows):
    position = lax.broadcasted_iota(i16, (16, LANES), 0)
    high = jnp.broadcast_to(index >> 7, (16, LANES)).astype(i16)
    low = jnp.broadcast_to(index & 127, (16, LANES)).astype(i16)
    one, zero = jnp.ones((), bf16), jnp.zeros((), bf16)
    masks = [position + jnp.int16(16 * step) == high for step in range(rows // 16)]
    upper = []
    for value in values:
        spread = jnp.broadcast_to(value, (16, LANES)).astype(bf16)
        upper.extend(jnp.where(mask, spread, zero) for mask in masks)
    lower = [jnp.where(position + jnp.int16(16 * step) == low, one, zero) for step in range(LANES // 16)]
    return jnp.concatenate(upper, 0), jnp.concatenate(lower, 0)


def halves(value):
    top = value.astype(bf16).astype(f32)
    return [top, value - top]


def sum_rows(pairs, rows):
    uppers, lowers = [], []
    for index, values in pairs:
        parts = [part for value in values for part in halves(value)]
        upper, lower = hot_rows(index, parts, rows)
        uppers.append(upper)
        lowers.append(lower)
    total = lax.dot_general(jnp.concatenate(uppers, 1), jnp.concatenate(lowers, 1), CONTRACT_LANES, preferred_element_type=f32)
    return [total[2 * n * rows:(2 * n + 1) * rows] + total[(2 * n + 1) * rows:(2 * n + 2) * rows] for n in range(len(pairs[0][1]))]


def pick(table_ref, index, rows):
    high, low = index >> 7, index & 127
    found = jnp.zeros((SUB, LANES), f32)
    for row in range(rows):
        line = jnp.broadcast_to(table_ref[row:row + 1, :], (SUB, LANES))
        found = jnp.where(high == row, jnp.take_along_axis(line, low, axis=1), found)
    return found


def tiles(n_rows, cap):
    return [(g, a) for g in range(n_rows // SUB) for a in range(cap // LANES)]


def at(g, a):
    return (pl.ds(g * SUB, SUB), pl.ds(a * LANES, LANES))


def lane_row(ref, r, a):
    return ref[r:r + 1, a * LANES:(a + 1) * LANES]


def whole_sum(x):
    return jnp.sum(jnp.sum(x, axis=1, keepdims=True), axis=0, keepdims=True)


def star_sums(star_ref, value_refs, n_rows, cap, sums_refs):
    for ref in sums_refs:
        ref[...] = jnp.zeros_like(ref)

    def block(g, carry):
        stars = star_ref[pl.ds(pl.multiple_of(g * SUB, SUB), SUB), :]
        values = [ref[pl.ds(pl.multiple_of(g * SUB, SUB), SUB), :] for ref in value_refs]
        pairs = []
        for r in range(SUB):
            for a in range(cap // LANES):
                cut = (slice(r, r + 1), slice(a * LANES, (a + 1) * LANES))
                pairs.append((stars[cut], [value[cut] for value in values]))
        for ref, part in zip(sums_refs, sum_rows(pairs, STAR_ROWS)):
            ref[...] += part
        return carry

    lax.fori_loop(0, n_rows // SUB, block, 0)


def first_terms(n_sky, count_ref, weight_ref, magnitude_ref, star_ref, terms_ref, live_ref, scale_ref, moment_ref, sums_ref, mean_ref):
    n_rows, cap = weight_ref.shape[2:]
    sub = lax.broadcasted_iota(jnp.int32, (SUB, LANES), 0)
    lane = lax.broadcasted_iota(jnp.int32, (SUB, LANES), 1)
    for g in range(n_rows // SUB):
        count = jnp.zeros((SUB, LANES), jnp.int32)
        for r in range(SUB):
            count = jnp.where(sub == r, count_ref[0, 0, g * SUB + r], count)
        for a in range(cap // LANES):
            where = at(g, a)
            live = jnp.where(lane + a * LANES < count, weight_ref[(0, 0) + where], 0.0)
            live_ref[where] = live
            moment_ref[where] = live * magnitude_ref[(0, 0) + where]
    star_sums(star_ref.at[0, 0], [live_ref, moment_ref], n_rows, cap, [scale_ref, sums_ref])
    scale_ref[...] = 1.0 / (prior + scale_ref[...])
    mean_ref[...] = sums_ref[...] * scale_ref[...]
    for g in range(n_rows // SUB):
        for a in range(cap // LANES):
            where = at(g, a)
            mean = pick(mean_ref, star_ref[(0, 0) + where], STAR_ROWS)
            term = live_ref[where] * (magnitude_ref[(0, 0) + where] - mean)
            for i in range(n_sky):
                terms_ref[i * n_rows + g * SUB:i * n_rows + (g + 1) * SUB, a, :] = term


def owner_sums(zp_ref, arrived, n_groups, cap, total_ref):
    total_ref[...] = jnp.zeros_like(total_ref)

    def block(g, carry):
        index = zp_ref[pl.ds(pl.multiple_of(g * SUB, SUB), SUB), :]
        pairs = []
        for r in range(SUB):
            for a in range(cap // LANES):
                pairs.append((index[r:r + 1, a * LANES:(a + 1) * LANES], [arrived(g, r, a)]))
        total_ref[...] += sum_rows(pairs, ZP_ROWS)[0]
        return carry

    lax.fori_loop(0, n_groups, block, 0)


def send_picks(zp_ref, table_ref, out_ref, scalar):
    n_rows, cap = zp_ref.shape[2:]
    for g in range(n_rows // SUB):

        def one(a, carry, g=g):
            lanes = pl.ds(pl.multiple_of(a * LANES, LANES), LANES)
            index = zp_ref[0, 0, g * SUB:(g + 1) * SUB, lanes]
            out_ref[g * SUB:(g + 1) * SUB, pl.ds(a, 1), :] = pick(table_ref, index, ZP_ROWS).reshape(SUB, 1, LANES)
            return carry

        lax.fori_loop(0, cap // LANES, one, 0, unroll=2)
    out_ref[:, cap // LANES, :] = jnp.broadcast_to(scalar, (n_rows, LANES))


def first_owner(n_sky, me_ref, arrived_ref, *refs):
    zp_refs, (sent_ref, all_ref, right_ref) = refs[:n_sky], refs[n_sky:]
    n_rows, cap = zp_refs[0].shape[2:]
    for d in range(n_sky):
        start = pl.multiple_of((me_ref[0] ^ d) * n_rows, SUB)
        all_ref[pl.ds(start, n_rows), :] = zp_refs[d][0, 0]

    def arrived(g, r, a):
        return arrived_ref[pl.ds(g * SUB + r, 1), a, :]

    owner_sums(all_ref, arrived, n_sky * n_rows // SUB, cap, right_ref)
    right = right_ref[...]
    send_picks(zp_refs[0], right_ref, sent_ref, whole_sum(right * right))


def star_terms(n_sky, star_ref, live_ref, scale_ref, slot_ref, product_ref, sums_ref, mean_ref, emit):
    n_rows, cap = live_ref.shape
    for g, a in tiles(n_rows, cap):
        product_ref[at(g, a)] = live_ref[at(g, a)] * slot_ref[at(g, a)]
    star_sums(star_ref.at[0, 0], [product_ref], n_rows, cap, [sums_ref])
    mean_ref[...] = sums_ref[...] * scale_ref[...]
    along = jnp.zeros((SUB, LANES), f32)
    for g, a in tiles(n_rows, cap):
        where = at(g, a)
        mean = pick(mean_ref, star_ref[(0, 0) + where], STAR_ROWS)
        slot = slot_ref[where]
        term = live_ref[where] * (slot - mean)
        along = along + slot * term
        emit(g, a, term)
    return whole_sum(along)


def second_terms(n_sky, values_ref, star_ref, live_ref, scale_ref, terms_ref, slot_ref, product_ref, sums_ref, mean_ref):
    n_rows, cap = live_ref.shape
    for g, a in tiles(n_rows, cap):
        slot_ref[at(g, a)] = values_ref[g * SUB:(g + 1) * SUB, a, :]

    def emit(g, a, term):
        for i in range(n_sky):
            terms_ref[i * n_rows + g * SUB:i * n_rows + (g + 1) * SUB, a, :] = term

    star_terms(n_sky, star_ref, live_ref, scale_ref, slot_ref, product_ref, sums_ref, mean_ref, emit)


def second_owner(arrived_ref, all_ref, right_ref, zp_ref, sent_ref, image_ref):
    n_rows, cap = zp_ref.shape[2:]

    def arrived(g, r, a):
        return arrived_ref[pl.ds(g * SUB + r, 1), a, :]

    owner_sums(all_ref, arrived, all_ref.shape[0] // SUB, cap, image_ref)
    right = right_ref[...]
    image_ref[...] = image_ref[...] + ridge * right
    send_picks(zp_ref, image_ref, sent_ref, whole_sum(right * image_ref[...]))


def third_terms(n_sky, first_ref, second_ref, star_ref, live_ref, scale_ref, right_ref, image_ref,
                terms_ref, residual_ref, scalar_ref, slot_ref, product_ref, sums_ref, mean_ref):
    n_rows, cap = live_ref.shape
    extra = cap // LANES
    norm = jnp.sum(first_ref[:, extra, :], axis=0, keepdims=True)
    product = jnp.sum(second_ref[:, extra, :], axis=0, keepdims=True)
    alpha = norm / product
    scalar_ref[0:1, :] = norm
    scalar_ref[1:2, :] = alpha
    residual = right_ref[...] - alpha * image_ref[...]
    residual_ref[...] = residual
    square = whole_sum(residual * residual)
    for g, a in tiles(n_rows, cap):
        rows = slice(g * SUB, (g + 1) * SUB)
        slot_ref[at(g, a)] = first_ref[rows, a, :] - alpha * second_ref[rows, a, :]

    def emit(g, a, term):
        for i in range(n_sky):
            terms_ref[i * n_rows + g * SUB:i * n_rows + (g + 1) * SUB, a * LANES:(a + 1) * LANES] = term

    along = star_terms(n_sky, star_ref, live_ref, scale_ref, slot_ref, product_ref, sums_ref, mean_ref, emit)
    lane = lax.broadcasted_iota(jnp.int32, (1, LANES), 1)
    both = jnp.where(lane < LANES // 2, along, square * (1.0 / n_sky))
    terms_ref[:, cap:cap + LANES] = jnp.broadcast_to(both, (n_sky * n_rows, LANES))


def last_owner(arrived_ref, all_ref, right_ref, image_ref, residual_ref, scalar_ref, points_ref, left_ref, total_ref):
    cap = all_ref.shape[1]

    def arrived(g, r, a):
        return arrived_ref[pl.ds(pl.multiple_of(g * SUB, SUB), SUB), a * LANES:(a + 1) * LANES][r:r + 1]

    owner_sums(all_ref, arrived, all_ref.shape[0] // SUB, cap, total_ref)
    sums = jnp.sum(arrived_ref[:, cap:cap + LANES], axis=0, keepdims=True)
    norm_next = sums[:, LANES // 2:LANES // 2 + 1]
    product = sums[:, 0:1] + ridge * norm_next
    norm, alpha = scalar_ref[0:1, 0:1], scalar_ref[1:2, 0:1]
    ratio = norm_next / norm
    step = norm_next / (product - ratio * norm_next / alpha)
    right, residual = right_ref[...], residual_ref[...]
    direction = residual + ratio * right
    along = (total_ref[...] + ridge * residual) + ratio * image_ref[...]
    points_ref[...] = alpha * right + step * direction
    left_ref[...] = residual - step * along


def call(kernel, shapes, scratch=(), flops=2_000_000, **more):
    return pl.pallas_call(
        kernel,
        out_shape=[jax.ShapeDtypeStruct(shape, f32) for shape in shapes],
        scratch_shapes=[pltpu.VMEM(shape, f32) for shape in scratch],
        compiler_params=pltpu.CompilerParams(vmem_limit_bytes=40 << 20),
        cost_estimate=pl.CostEstimate(flops=flops * 1000, bytes_accessed=1 << 20, transcendentals=0),
        **more,
    )


def body(obs_weight, magnitude, star_id, peer_count, zp_index):
    n_sky, n_exp = lax.axis_size("sky"), lax.axis_size("exp")
    cap = obs_weight.shape[3]
    tall, star, slots = (ZP_ROWS, LANES), (STAR_ROWS, LANES), (n_exp, cap)
    terms = (n_sky * n_exp, cap // LANES, LANES)
    picks = (n_exp, 2 * SUB, LANES)
    vmem = pl.BlockSpec(memory_space=pltpu.VMEM)
    smem = pl.BlockSpec(memory_space=pltpu.SMEM)
    me = jnp.reshape(lax.axis_index("sky"), (1,)).astype(jnp.int32)

    def to_owners(x):
        return lax.all_to_all(x, ("sky", "exp"), split_axis=0, concat_axis=0, tiled=True)

    def to_sources(x):
        return lax.all_to_all(x, "exp", split_axis=0, concat_axis=0, tiled=True)

    zp = [zp_index] + [lax.ppermute(zp_index, "sky", [(i, i ^ d) for i in range(n_sky)]) for d in range(1, n_sky)]
    sent, live, scale = call(
        functools.partial(first_terms, n_sky), [terms, slots, star], [slots, star, star],
        in_specs=[smem, vmem, vmem, vmem],
    )(peer_count, obs_weight, magnitude, star_id)
    arrived = to_owners(sent)
    sent, zp_all, right = pl.pallas_call(
        functools.partial(first_owner, n_sky),
        out_shape=[jax.ShapeDtypeStruct(picks, f32), jax.ShapeDtypeStruct((n_sky * n_exp, cap), jnp.int32), jax.ShapeDtypeStruct(tall, f32)],
        in_specs=[smem] + [vmem] * (n_sky + 1),
        compiler_params=pltpu.CompilerParams(vmem_limit_bytes=40 << 20),
    )(me, arrived, *zp)
    first = to_sources(sent)
    (sent,) = call(functools.partial(second_terms, n_sky), [terms], [slots, slots, star, star])(first, star_id, live, scale)
    arrived = to_owners(sent)
    sent, image = call(second_owner, [picks, tall])(arrived, zp_all, right, zp_index)
    second = to_sources(sent)
    sent, residual, scalars = call(
        functools.partial(third_terms, n_sky), [(n_sky * n_exp, cap + LANES), tall, (SUB, LANES)], [slots, slots, star, star]
    )(first, second, star_id, live, scale, right, image)
    arrived = to_owners(sent)
    points, left = call(last_owner, [tall, tall], [tall])(arrived, zp_all, right, image, residual, scalars)
    return points.reshape(-1)[:ZP_DEV], left.reshape(-1)[:ZP_DEV]


def solution(mesh):
    return jax.shard_map(
        body,
        mesh=mesh,
        in_specs=(
            P("sky", "exp", None, None),
            P("sky", "exp", None, None),
            P("sky", "exp", None, None),
            P("sky", "exp", None),
            P("sky", "exp", None, None),
        ),
        out_specs=(P("exp"), P("exp")),
        check_vma=False,
    )
```

```python
import functools

import jax
import jax.numpy as jnp
from jax import lax
from jax.experimental import pallas as pl
from jax.experimental.pallas import tpu as pltpu
from jax.sharding import PartitionSpec as P

STAR_DEV = 4096
ZP_DEV = 12096
LANES = 128
SUB = 8
ridge = 1.0
prior = 1.0

f32 = jnp.float32
bf16 = jnp.bfloat16
i16 = jnp.int16
STAR_ROWS = STAR_DEV // LANES
ZP_ROWS = -(-ZP_DEV // (LANES * 16)) * 16
WIDE_ROWS, WIDE_COLUMNS = 64, 192


def hot_rows(upper_index, lower_index, values, rows, columns):
    position = lax.broadcasted_iota(i16, (16, LANES), 0)
    high = jnp.broadcast_to(upper_index, (16, LANES)).astype(i16)
    one, zero = jnp.ones((), bf16), jnp.zeros((), bf16)
    masks = [position + jnp.int16(16 * step) == high for step in range(rows // 16)]
    upper = []
    for value in values:
        spread = jnp.broadcast_to(value, (16, LANES)).astype(bf16)
        upper.extend(jnp.where(mask, spread, zero) for mask in masks)
    low = jnp.broadcast_to(lower_index.astype(f32), (LANES, LANES)).astype(bf16).T
    lane = lax.broadcasted_iota(jnp.int32, (LANES, LANES), 1).astype(f32).astype(bf16)
    lower = [
        jnp.where(low == lane + jnp.asarray(start, bf16), one, zero)[:, :min(LANES, columns - start)]
        for start in range(0, columns, LANES)
    ]
    return jnp.concatenate(upper, 0), jnp.concatenate(lower, 1)


def halves(value):
    top = value.astype(bf16).astype(f32)
    return [top, value - top]


def sum_rows(entries, rows, columns):
    uppers, lowers = [], []
    for upper_index, lower_index, values in entries:
        parts = [part for value in values for part in halves(value)]
        upper, lower = hot_rows(upper_index, lower_index, parts, rows, columns)
        uppers.append(upper)
        lowers.append(lower)
    total = jnp.dot(jnp.concatenate(uppers, 1), jnp.concatenate(lowers, 0), preferred_element_type=f32)
    return [total[2 * n * rows:(2 * n + 1) * rows] + total[(2 * n + 1) * rows:(2 * n + 2) * rows] for n in range(len(entries[0][2]))]


def pick(table_ref, index, rows):
    high, low = index >> 7, index & 127
    found = jnp.zeros((SUB, LANES), f32)
    for row in range(rows):
        line = jnp.broadcast_to(table_ref[row:row + 1, :], (SUB, LANES))
        found = jnp.where(high == row, jnp.take_along_axis(line, low, axis=1), found)
    return found


def tiles(n_rows, cap):
    return [(g, a) for g in range(n_rows // SUB) for a in range(cap // LANES)]


def at(g, a):
    return (pl.ds(g * SUB, SUB), pl.ds(a * LANES, LANES))


def lane_row(ref, r, a):
    return ref[r:r + 1, a * LANES:(a + 1) * LANES]


def whole_sum(x):
    return jnp.sum(jnp.sum(x, axis=1, keepdims=True), axis=0, keepdims=True)


def star_sums(star_ref, value_refs, n_rows, cap, sums_refs):
    for ref in sums_refs:
        ref[...] = jnp.zeros_like(ref)

    def block(g, carry):
        stars = star_ref[pl.ds(pl.multiple_of(g * SUB, SUB), SUB), :]
        values = [ref[pl.ds(pl.multiple_of(g * SUB, SUB), SUB), :] for ref in value_refs]
        high, low = stars >> 7, stars & 127
        pairs = []
        for r in range(SUB):
            for a in range(cap // LANES):
                cut = (slice(r, r + 1), slice(a * LANES, (a + 1) * LANES))
                pairs.append((high[cut], low[cut], [value[cut] for value in values]))
        for ref, part in zip(sums_refs, sum_rows(pairs, STAR_ROWS, LANES)):
            ref[...] += part
        return carry

    lax.fori_loop(0, n_rows // SUB, block, 0)


def first_terms(n_sky, count_ref, weight_from, magnitude_from, star_from, terms_ref, live_ref, scale_ref,
                weight_ref, magnitude_ref, star_ref, moment_ref, sums_ref, mean_ref, arrival):
    n_rows, cap = weight_from.shape[2:]
    copies = [
        pltpu.make_async_copy(source, target, arrival.at[n])
        for n, (source, target) in enumerate(
            [(weight_from, weight_ref), (magnitude_from, magnitude_ref), (star_from, star_ref)])
    ]
    for copy in copies:
        copy.start()
    for copy in copies:
        copy.wait()
    sub = lax.broadcasted_iota(jnp.int32, (SUB, LANES), 0)
    lane = lax.broadcasted_iota(jnp.int32, (SUB, LANES), 1)
    for g in range(n_rows // SUB):
        count = jnp.zeros((SUB, LANES), jnp.int32)
        for r in range(SUB):
            count = jnp.where(sub == r, count_ref[0, 0, g * SUB + r], count)
        for a in range(cap // LANES):
            where = at(g, a)
            live = jnp.where(lane + a * LANES < count, weight_ref[(0, 0) + where], 0.0)
            live_ref[where] = live
            moment_ref[where] = live * magnitude_ref[(0, 0) + where]
    star_sums(star_ref.at[0, 0], [live_ref, moment_ref], n_rows, cap, [scale_ref, sums_ref])
    scale_ref[...] = 1.0 / (prior + scale_ref[...])
    mean_ref[...] = sums_ref[...] * scale_ref[...]
    for g in range(n_rows // SUB):
        for a in range(cap // LANES):
            where = at(g, a)
            mean = pick(mean_ref, star_ref[(0, 0) + where], STAR_ROWS)
            term = live_ref[where] * (magnitude_ref[(0, 0) + where] - mean)
            for i in range(n_sky):
                terms_ref[i * n_rows + g * SUB:i * n_rows + (g + 1) * SUB, a, :] = term


def owner_sums(zp_ref, arrived, n_groups, cap, total_ref, wide_ref):
    wide_ref[...] = jnp.zeros_like(wide_ref)

    def block(g, carry):
        index = zp_ref[pl.ds(pl.multiple_of(g * SUB, SUB), SUB), :]
        row, lane = index >> 7, index & 127
        beyond = row >= WIDE_ROWS
        high = jnp.where(beyond, row - WIDE_ROWS + ((lane >> 6) << 5), row)
        low = jnp.where(beyond, LANES + (lane & 63), lane)
        pairs = []
        for r in range(SUB):
            for a in range(cap // LANES):
                cut = (slice(r, r + 1), slice(a * LANES, (a + 1) * LANES))
                pairs.append((high[cut], low[cut], [arrived(g, r, a)]))
        wide_ref[...] += sum_rows(pairs, WIDE_ROWS, WIDE_COLUMNS)[0]
        return carry

    lax.fori_loop(0, n_groups, block, 0)
    total_ref[0:WIDE_ROWS, :] = wide_ref[:, 0:LANES]
    total_ref[WIDE_ROWS:ZP_ROWS, :] = jnp.concatenate(
        [wide_ref[0:WIDE_ROWS // 2, LANES:WIDE_COLUMNS], wide_ref[WIDE_ROWS // 2:WIDE_ROWS, LANES:WIDE_COLUMNS]], 1)


def send_picks(zp_ref, table_ref, out_ref, scalar):
    n_rows, cap = zp_ref.shape[2:]
    for g in range(n_rows // SUB):
        rows = slice(g * SUB, (g + 1) * SUB)
        for a in range(cap // LANES):
            index = zp_ref[0, 0, rows, a * LANES:(a + 1) * LANES]
            out_ref[rows, a, :] = pick(table_ref, index, ZP_ROWS)
    out_ref[:, cap // LANES, :] = jnp.broadcast_to(scalar, (n_rows, LANES))


def first_owner(n_sky, me_ref, arrived_ref, *refs):
    zp_refs, (sent_ref, all_ref, right_ref, wide_ref) = refs[:n_sky], refs[n_sky:]
    n_rows, cap = zp_refs[0].shape[2:]
    for d in range(n_sky):
        start = pl.multiple_of((me_ref[0] ^ d) * n_rows, SUB)
        all_ref[pl.ds(start, n_rows), :] = zp_refs[d][0, 0]

    def arrived(g, r, a):
        return arrived_ref[pl.ds(g * SUB + r, 1), a, :]

    owner_sums(all_ref, arrived, n_sky * n_rows // SUB, cap, right_ref, wide_ref)
    right = right_ref[...]
    send_picks(zp_refs[0], right_ref, sent_ref, whole_sum(right * right))


def star_terms(n_sky, star_ref, live_ref, scale_ref, slot_ref, product_ref, sums_ref, mean_ref, emit):
    n_rows, cap = live_ref.shape
    for g, a in tiles(n_rows, cap):
        product_ref[at(g, a)] = live_ref[at(g, a)] * slot_ref[at(g, a)]
    star_sums(star_ref.at[0, 0], [product_ref], n_rows, cap, [sums_ref])
    mean_ref[...] = sums_ref[...] * scale_ref[...]
    along = jnp.zeros((SUB, LANES), f32)
    for g, a in tiles(n_rows, cap):
        where = at(g, a)
        mean = pick(mean_ref, star_ref[(0, 0) + where], STAR_ROWS)
        slot = slot_ref[where]
        term = live_ref[where] * (slot - mean)
        along = along + slot * term
        emit(g, a, term)
    return whole_sum(along)


def second_terms(n_sky, values_ref, star_ref, live_ref, scale_ref, terms_ref, slot_ref, product_ref, sums_ref, mean_ref):
    n_rows, cap = live_ref.shape
    for g, a in tiles(n_rows, cap):
        slot_ref[at(g, a)] = values_ref[g * SUB:(g + 1) * SUB, a, :]

    def emit(g, a, term):
        for i in range(n_sky):
            terms_ref[i * n_rows + g * SUB:i * n_rows + (g + 1) * SUB, a, :] = term

    star_terms(n_sky, star_ref, live_ref, scale_ref, slot_ref, product_ref, sums_ref, mean_ref, emit)


def second_owner(arrived_ref, all_ref, right_ref, zp_ref, sent_ref, image_ref, wide_ref):
    n_rows, cap = zp_ref.shape[2:]

    def arrived(g, r, a):
        return arrived_ref[pl.ds(g * SUB + r, 1), a, :]

    owner_sums(all_ref, arrived, all_ref.shape[0] // SUB, cap, image_ref, wide_ref)
    right = right_ref[...]
    image_ref[...] = image_ref[...] + ridge * right
    send_picks(zp_ref, image_ref, sent_ref, whole_sum(right * image_ref[...]))


def third_terms(n_sky, first_ref, second_ref, star_ref, live_ref, scale_ref, right_ref, image_ref,
                terms_ref, residual_ref, scalar_ref, slot_ref, product_ref, sums_ref, mean_ref):
    n_rows, cap = live_ref.shape
    extra = cap // LANES
    norm = jnp.sum(first_ref[:, extra, :], axis=0, keepdims=True)
    product = jnp.sum(second_ref[:, extra, :], axis=0, keepdims=True)
    alpha = norm / product
    scalar_ref[0:1, :] = norm
    scalar_ref[1:2, :] = alpha
    residual = right_ref[...] - alpha * image_ref[...]
    residual_ref[...] = residual
    square = whole_sum(residual * residual)
    for g, a in tiles(n_rows, cap):
        rows = slice(g * SUB, (g + 1) * SUB)
        slot_ref[at(g, a)] = first_ref[rows, a, :] - alpha * second_ref[rows, a, :]

    def emit(g, a, term):
        for i in range(n_sky):
            terms_ref[i * n_rows + g * SUB:i * n_rows + (g + 1) * SUB, a * LANES:(a + 1) * LANES] = term

    along = star_terms(n_sky, star_ref, live_ref, scale_ref, slot_ref, product_ref, sums_ref, mean_ref, emit)
    lane = lax.broadcasted_iota(jnp.int32, (1, LANES), 1)
    both = jnp.where(lane < LANES // 2, along, square * (1.0 / n_sky))
    terms_ref[:, cap:cap + LANES] = jnp.broadcast_to(both, (n_sky * n_rows, LANES))


def last_owner(arrived_ref, all_ref, right_ref, image_ref, residual_ref, scalar_ref, points_ref, left_ref, total_ref, wide_ref):
    cap = all_ref.shape[1]

    def arrived(g, r, a):
        return arrived_ref[pl.ds(pl.multiple_of(g * SUB, SUB), SUB), a * LANES:(a + 1) * LANES][r:r + 1]

    owner_sums(all_ref, arrived, all_ref.shape[0] // SUB, cap, total_ref, wide_ref)
    sums = jnp.sum(arrived_ref[:, cap:cap + LANES], axis=0, keepdims=True)
    norm_next = sums[:, LANES // 2:LANES // 2 + 1]
    product = sums[:, 0:1] + ridge * norm_next
    norm, alpha = scalar_ref[0:1, 0:1], scalar_ref[1:2, 0:1]
    ratio = norm_next / norm
    step = norm_next / (product - ratio * norm_next / alpha)
    right, residual = right_ref[...], residual_ref[...]
    direction = residual + ratio * right
    along = (total_ref[...] + ridge * residual) + ratio * image_ref[...]
    points_ref[...] = alpha * right + step * direction
    left_ref[...] = residual - step * along


def call(kernel, shapes, scratch=(), flops=2_000_000, **more):
    return pl.pallas_call(
        kernel,
        out_shape=[jax.ShapeDtypeStruct(shape, f32) for shape in shapes],
        scratch_shapes=[pltpu.VMEM(shape, f32) for shape in scratch],
        compiler_params=pltpu.CompilerParams(vmem_limit_bytes=40 << 20),
        cost_estimate=pl.CostEstimate(flops=flops * 1000, bytes_accessed=1 << 20, transcendentals=0),
        **more,
    )


def body(obs_weight, magnitude, star_id, peer_count, zp_index):
    n_sky, n_exp = lax.axis_size("sky"), lax.axis_size("exp")
    cap = obs_weight.shape[3]
    tall, star, slots = (ZP_ROWS, LANES), (STAR_ROWS, LANES), (n_exp, cap)
    terms = (n_sky * n_exp, cap // LANES, LANES)
    picks = (n_exp, 2 * SUB, LANES)
    wide = (WIDE_ROWS, WIDE_COLUMNS)
    vmem = pl.BlockSpec(memory_space=pltpu.VMEM)
    smem = pl.BlockSpec(memory_space=pltpu.SMEM)
    me = jnp.reshape(lax.axis_index("sky"), (1,)).astype(jnp.int32)

    def to_owners(x):
        return lax.all_to_all(x, ("sky", "exp"), split_axis=0, concat_axis=0, tiled=True)

    def to_sources(x):
        return lax.all_to_all(x, "exp", split_axis=0, concat_axis=0, tiled=True)

    zp = [zp_index] + [lax.ppermute(zp_index, "sky", [(i, i ^ d) for i in range(n_sky)]) for d in range(1, n_sky)]
    anywhere = pl.BlockSpec(memory_space=pl.ANY)
    whole = (1, 1, n_exp, cap)
    sent, live, scale = pl.pallas_call(
        functools.partial(first_terms, n_sky),
        out_shape=[jax.ShapeDtypeStruct(shape, f32) for shape in (terms, slots, star)],
        in_specs=[smem, anywhere, anywhere, anywhere],
        scratch_shapes=[pltpu.VMEM(whole, f32), pltpu.VMEM(whole, f32), pltpu.VMEM(whole, jnp.int32),
                        pltpu.VMEM(slots, f32), pltpu.VMEM(star, f32), pltpu.VMEM(star, f32), pltpu.SemaphoreType.DMA((3,))],
        compiler_params=pltpu.CompilerParams(vmem_limit_bytes=58 << 20),
        cost_estimate=pl.CostEstimate(flops=2_000_000_000, bytes_accessed=1 << 20, transcendentals=0),
    )(peer_count, obs_weight, magnitude, star_id)
    arrived = to_owners(sent)
    sent, zp_all, right = pl.pallas_call(
        functools.partial(first_owner, n_sky),
        out_shape=[jax.ShapeDtypeStruct(picks, f32), jax.ShapeDtypeStruct((n_sky * n_exp, cap), jnp.int32), jax.ShapeDtypeStruct(tall, f32)],
        in_specs=[smem] + [vmem] * (n_sky + 1),
        scratch_shapes=[pltpu.VMEM(wide, f32)],
        compiler_params=pltpu.CompilerParams(vmem_limit_bytes=40 << 20),
    )(me, arrived, *zp)
    first = to_sources(sent)
    (sent,) = call(functools.partial(second_terms, n_sky), [terms], [slots, slots, star, star])(first, star_id, live, scale)
    arrived = to_owners(sent)
    sent, image = call(second_owner, [picks, tall], [wide])(arrived, zp_all, right, zp_index)
    second = to_sources(sent)
    sent, residual, scalars = call(
        functools.partial(third_terms, n_sky), [(n_sky * n_exp, cap + LANES), tall, (SUB, LANES)], [slots, slots, star, star]
    )(first, second, star_id, live, scale, right, image)
    arrived = to_owners(sent)
    points, left = call(last_owner, [tall, tall], [tall, wide])(arrived, zp_all, right, image, residual, scalars)
    return points.reshape(-1)[:ZP_DEV], left.reshape(-1)[:ZP_DEV]


def solution(mesh):
    return jax.shard_map(
        body,
        mesh=mesh,
        in_specs=(
            P("sky", "exp", None, None),
            P("sky", "exp", None, None),
            P("sky", "exp", None, None),
            P("sky", "exp", None),
            P("sky", "exp", None, None),
        ),
        out_specs=(P("exp"), P("exp")),
        check_vma=False,
    )
```

```python
import functools
import math

import jax
import jax.numpy as jnp
from jax import lax
from jax.experimental import pallas as pl
from jax.experimental.pallas import tpu as pltpu
from jax.sharding import PartitionSpec as P

STAR_DEV = 4096
ZP_DEV = 12096
LANES = 128
SUB = 8
ridge = 1.0
prior = 1.0

f32 = jnp.float32
bf16 = jnp.bfloat16
i16 = jnp.int16
STAR_ROWS = STAR_DEV // LANES
ZP_ROWS = -(-ZP_DEV // (LANES * 16)) * 16
HALF_ROWS = ZP_ROWS // 2
OWNER_BLOCK = 32


def hot_rows(upper_index, lower_index, values, rows, columns):
    position = lax.broadcasted_iota(i16, (16, LANES), 0)
    high = jnp.broadcast_to(upper_index, (16, LANES)).astype(i16)
    one, zero = jnp.ones((), bf16), jnp.zeros((), bf16)
    masks = [position + jnp.int16(16 * step) == high for step in range(rows // 16)]
    upper = []
    for value in values:
        spread = jnp.broadcast_to(value, (16, LANES)).astype(bf16)
        upper.extend(jnp.where(mask, spread, zero) for mask in masks)
    low = jnp.broadcast_to(lower_index.astype(f32), (LANES, LANES)).astype(bf16).T
    lane = lax.broadcasted_iota(jnp.int32, (LANES, LANES), 1).astype(f32).astype(bf16)
    lower = [
        jnp.where(low == lane + jnp.asarray(start, bf16), one, zero)[:, :min(LANES, columns - start)]
        for start in range(0, columns, LANES)
    ]
    return jnp.concatenate(upper, 0), jnp.concatenate(lower, 1)


def halves(value):
    top = value.astype(bf16).astype(f32)
    return [top, value - top]


def sum_rows(entries, rows, columns):
    uppers, lowers = [], []
    for upper_index, lower_index, values in entries:
        parts = [part for value in values for part in halves(value)]
        upper, lower = hot_rows(upper_index, lower_index, parts, rows, columns)
        uppers.append(upper)
        lowers.append(lower)
    total = jnp.dot(jnp.concatenate(uppers, 1), jnp.concatenate(lowers, 0), preferred_element_type=f32)
    return [total[2 * n * rows:(2 * n + 1) * rows] + total[(2 * n + 1) * rows:(2 * n + 2) * rows] for n in range(len(entries[0][2]))]


def pick(table_ref, index, rows):
    high, low = index >> 7, index & 127
    found = jnp.zeros((SUB, LANES), f32)
    for row in range(rows):
        line = jnp.broadcast_to(table_ref[row:row + 1, :], (SUB, LANES))
        found = jnp.where(high == row, jnp.take_along_axis(line, low, axis=1), found)
    return found


def tiles(n_rows, cap):
    return [(g, a) for g in range(n_rows // SUB) for a in range(cap // LANES)]


def at(g, a):
    return (pl.ds(g * SUB, SUB), pl.ds(a * LANES, LANES))


def lane_row(ref, r, a):
    return ref[r:r + 1, a * LANES:(a + 1) * LANES]


def whole_sum(x):
    return jnp.sum(jnp.sum(x, axis=1, keepdims=True), axis=0, keepdims=True)


def star_sums(star_ref, value_refs, n_rows, cap, sums_refs):
    for ref in sums_refs:
        ref[...] = jnp.zeros_like(ref)

    def block(g, carry):
        stars = star_ref[pl.ds(pl.multiple_of(g * SUB, SUB), SUB), :]
        values = [ref[pl.ds(pl.multiple_of(g * SUB, SUB), SUB), :] for ref in value_refs]
        high, low = stars >> 7, stars & 127
        pairs = []
        for r in range(SUB):
            for a in range(cap // LANES):
                cut = (slice(r, r + 1), slice(a * LANES, (a + 1) * LANES))
                pairs.append((high[cut], low[cut], [value[cut] for value in values]))
        for ref, part in zip(sums_refs, sum_rows(pairs, STAR_ROWS, LANES)):
            ref[...] += part
        return carry

    lax.fori_loop(0, n_rows // SUB, block, 0)


def first_terms(n_sky, count_ref, weight_from, magnitude_from, star_from, terms_ref, live_ref, scale_ref,
                weight_ref, magnitude_ref, star_ref, moment_ref, sums_ref, mean_ref, arrival):
    n_rows, cap = weight_from.shape[2:]
    copies = [
        pltpu.make_async_copy(source, target, arrival.at[n])
        for n, (source, target) in enumerate(
            [(weight_from, weight_ref), (magnitude_from, magnitude_ref), (star_from, star_ref)])
    ]
    for copy in copies:
        copy.start()
    for copy in copies:
        copy.wait()
    sub = lax.broadcasted_iota(jnp.int32, (SUB, LANES), 0)
    lane = lax.broadcasted_iota(jnp.int32, (SUB, LANES), 1)
    for g in range(n_rows // SUB):
        count = jnp.zeros((SUB, LANES), jnp.int32)
        for r in range(SUB):
            count = jnp.where(sub == r, count_ref[0, 0, g * SUB + r], count)
        for a in range(cap // LANES):
            where = at(g, a)
            live = jnp.where(lane + a * LANES < count, weight_ref[(0, 0) + where], 0.0)
            live_ref[where] = live
            moment_ref[where] = live * magnitude_ref[(0, 0) + where]
    star_sums(star_ref.at[0, 0], [live_ref, moment_ref], n_rows, cap, [scale_ref, sums_ref])
    scale_ref[...] = 1.0 / (prior + scale_ref[...])
    mean_ref[...] = sums_ref[...] * scale_ref[...]
    for g in range(n_rows // SUB):
        for a in range(cap // LANES):
            where = at(g, a)
            mean = pick(mean_ref, star_ref[(0, 0) + where], STAR_ROWS)
            term = live_ref[where] * (magnitude_ref[(0, 0) + where] - mean)
            for i in range(n_sky):
                terms_ref[i * n_rows + g * SUB:i * n_rows + (g + 1) * SUB, a, :] = term


def owner_sums(zp_ref, arrived, n_rows, cap, total_ref, most=OWNER_BLOCK):
    total_ref[...] = jnp.zeros_like(total_ref)
    step = math.gcd(n_rows, most)

    def block(n, carry):
        entries = []
        for g in range(step // SUB):
            first = pl.multiple_of(n * step + g * SUB, SUB)
            index = zp_ref[pl.ds(first, SUB), :]
            row, lane = index >> 7, index & 127
            beyond = row >= HALF_ROWS
            high = jnp.where(beyond, row - HALF_ROWS, row)
            low = jnp.where(beyond, lane + LANES, lane)
            for r in range(SUB):
                for a in range(cap // LANES):
                    cut = (slice(r, r + 1), slice(a * LANES, (a + 1) * LANES))
                    entries.append((high[cut], low[cut], [arrived(first, r, a)]))
        total = sum_rows(entries, HALF_ROWS, 2 * LANES)[0]
        total_ref[0:HALF_ROWS, :] += total[:, 0:LANES]
        total_ref[HALF_ROWS:ZP_ROWS, :] += total[:, LANES:2 * LANES]
        return carry

    lax.fori_loop(0, n_rows // step, block, 0)


def send_picks(zp_ref, table_ref, out_ref, scalar):
    n_rows, cap = zp_ref.shape[2:]
    for g in range(n_rows // SUB):
        rows = slice(g * SUB, (g + 1) * SUB)

        def one(a, carry, rows=rows):
            lanes = pl.ds(pl.multiple_of(a * LANES, LANES), LANES)
            index = zp_ref[0, 0, rows, lanes]
            out_ref[rows, pl.ds(a, 1), :] = pick(table_ref, index, ZP_ROWS).reshape(SUB, 1, LANES)
            return carry

        lax.fori_loop(0, cap // LANES, one, 0, unroll=4)
    out_ref[:, cap // LANES, :] = jnp.broadcast_to(scalar, (n_rows, LANES))


def first_owner(n_sky, me_ref, arrived_ref, *refs):
    zp_refs, (sent_ref, all_ref, right_ref) = refs[:n_sky], refs[n_sky:]
    n_rows, cap = zp_refs[0].shape[2:]
    for d in range(n_sky):
        start = pl.multiple_of((me_ref[0] ^ d) * n_rows, SUB)
        all_ref[pl.ds(start, n_rows), :] = zp_refs[d][0, 0]

    def arrived(first, r, a):
        return arrived_ref[pl.ds(first + r, 1), a, :]

    owner_sums(all_ref, arrived, n_sky * n_rows, cap, right_ref, 32)
    right = right_ref[...]
    send_picks(zp_refs[0], right_ref, sent_ref, whole_sum(right * right))


def star_terms(n_sky, star_ref, live_ref, scale_ref, slot_ref, product_ref, sums_ref, mean_ref, emit):
    n_rows, cap = live_ref.shape
    for g, a in tiles(n_rows, cap):
        product_ref[at(g, a)] = live_ref[at(g, a)] * slot_ref[at(g, a)]
    star_sums(star_ref.at[0, 0], [product_ref], n_rows, cap, [sums_ref])
    mean_ref[...] = sums_ref[...] * scale_ref[...]
    along = jnp.zeros((SUB, LANES), f32)
    for g, a in tiles(n_rows, cap):
        where = at(g, a)
        mean = pick(mean_ref, star_ref[(0, 0) + where], STAR_ROWS)
        slot = slot_ref[where]
        term = live_ref[where] * (slot - mean)
        along = along + slot * term
        emit(g, a, term)
    return whole_sum(along)


def second_terms(n_sky, values_ref, star_ref, live_ref, scale_ref, terms_ref, slot_ref, product_ref, sums_ref, mean_ref):
    n_rows, cap = live_ref.shape
    for g, a in tiles(n_rows, cap):
        slot_ref[at(g, a)] = values_ref[g * SUB:(g + 1) * SUB, a, :]

    def emit(g, a, term):
        for i in range(n_sky):
            terms_ref[i * n_rows + g * SUB:i * n_rows + (g + 1) * SUB, a, :] = term

    star_terms(n_sky, star_ref, live_ref, scale_ref, slot_ref, product_ref, sums_ref, mean_ref, emit)


def second_owner(arrived_ref, all_ref, right_ref, zp_ref, sent_ref, image_ref):
    n_rows, cap = zp_ref.shape[2:]

    def arrived(first, r, a):
        return arrived_ref[pl.ds(first + r, 1), a, :]

    owner_sums(all_ref, arrived, all_ref.shape[0], cap, image_ref, 32)
    right = right_ref[...]
    image_ref[...] = image_ref[...] + ridge * right
    send_picks(zp_ref, image_ref, sent_ref, whole_sum(right * image_ref[...]))


def third_terms(n_sky, first_ref, second_ref, star_ref, live_ref, scale_ref, right_ref, image_ref,
                terms_ref, residual_ref, scalar_ref, slot_ref, product_ref, sums_ref, mean_ref):
    n_rows, cap = live_ref.shape
    extra = cap // LANES
    norm = jnp.sum(first_ref[:, extra, :], axis=0, keepdims=True)
    product = jnp.sum(second_ref[:, extra, :], axis=0, keepdims=True)
    alpha = norm / product
    scalar_ref[0:1, :] = norm
    scalar_ref[1:2, :] = alpha
    residual = right_ref[...] - alpha * image_ref[...]
    residual_ref[...] = residual
    square = whole_sum(residual * residual)
    for g, a in tiles(n_rows, cap):
        rows = slice(g * SUB, (g + 1) * SUB)
        slot_ref[at(g, a)] = first_ref[rows, a, :] - alpha * second_ref[rows, a, :]

    def emit(g, a, term):
        for i in range(n_sky):
            terms_ref[i * n_rows + g * SUB:i * n_rows + (g + 1) * SUB, a * LANES:(a + 1) * LANES] = term

    along = star_terms(n_sky, star_ref, live_ref, scale_ref, slot_ref, product_ref, sums_ref, mean_ref, emit)
    lane = lax.broadcasted_iota(jnp.int32, (1, LANES), 1)
    both = jnp.where(lane < LANES // 2, along, square * (1.0 / n_sky))
    terms_ref[:, cap:cap + LANES] = jnp.broadcast_to(both, (n_sky * n_rows, LANES))


def last_owner(arrived_ref, all_ref, right_ref, image_ref, residual_ref, scalar_ref, points_ref, left_ref, total_ref):
    cap = all_ref.shape[1]

    def arrived(first, r, a):
        return arrived_ref[pl.ds(first, SUB), a * LANES:(a + 1) * LANES][r:r + 1]

    owner_sums(all_ref, arrived, all_ref.shape[0], cap, total_ref)
    sums = jnp.sum(arrived_ref[:, cap:cap + LANES], axis=0, keepdims=True)
    norm_next = sums[:, LANES // 2:LANES // 2 + 1]
    product = sums[:, 0:1] + ridge * norm_next
    norm, alpha = scalar_ref[0:1, 0:1], scalar_ref[1:2, 0:1]
    ratio = norm_next / norm
    step = norm_next / (product - ratio * norm_next / alpha)
    right, residual = right_ref[...], residual_ref[...]
    direction = residual + ratio * right
    along = (total_ref[...] + ridge * residual) + ratio * image_ref[...]
    points_ref[...] = alpha * right + step * direction
    left_ref[...] = residual - step * along


def call(kernel, shapes, scratch=(), flops=2_000_000, **more):
    return pl.pallas_call(
        kernel,
        out_shape=[jax.ShapeDtypeStruct(shape, f32) for shape in shapes],
        scratch_shapes=[pltpu.VMEM(shape, f32) for shape in scratch],
        compiler_params=pltpu.CompilerParams(vmem_limit_bytes=40 << 20),
        cost_estimate=pl.CostEstimate(flops=flops * 1000, bytes_accessed=1 << 20, transcendentals=0),
        **more,
    )


def body(obs_weight, magnitude, star_id, peer_count, zp_index):
    n_sky, n_exp = lax.axis_size("sky"), lax.axis_size("exp")
    cap = obs_weight.shape[3]
    tall, star, slots = (ZP_ROWS, LANES), (STAR_ROWS, LANES), (n_exp, cap)
    terms = (n_sky * n_exp, cap // LANES, LANES)
    picks = (n_exp, 2 * SUB, LANES)
    vmem = pl.BlockSpec(memory_space=pltpu.VMEM)
    smem = pl.BlockSpec(memory_space=pltpu.SMEM)
    me = jnp.reshape(lax.axis_index("sky"), (1,)).astype(jnp.int32)

    def to_owners(x):
        return lax.all_to_all(x, ("sky", "exp"), split_axis=0, concat_axis=0, tiled=True)

    def to_sources(x):
        return lax.all_to_all(x, "exp", split_axis=0, concat_axis=0, tiled=True)

    zp = [zp_index] + [lax.ppermute(zp_index, "sky", [(i, i ^ d) for i in range(n_sky)]) for d in range(1, n_sky)]
    anywhere = pl.BlockSpec(memory_space=pl.ANY)
    whole = (1, 1, n_exp, cap)
    sent, live, scale = pl.pallas_call(
        functools.partial(first_terms, n_sky),
        out_shape=[jax.ShapeDtypeStruct(shape, f32) for shape in (terms, slots, star)],
        in_specs=[smem, anywhere, anywhere, anywhere],
        scratch_shapes=[pltpu.VMEM(whole, f32), pltpu.VMEM(whole, f32), pltpu.VMEM(whole, jnp.int32),
                        pltpu.VMEM(slots, f32), pltpu.VMEM(star, f32), pltpu.VMEM(star, f32), pltpu.SemaphoreType.DMA((3,))],
        compiler_params=pltpu.CompilerParams(vmem_limit_bytes=58 << 20),
        cost_estimate=pl.CostEstimate(flops=2_000_000_000, bytes_accessed=1 << 20, transcendentals=0),
    )(peer_count, obs_weight, magnitude, star_id)
    arrived = to_owners(sent)
    sent, zp_all, right = pl.pallas_call(
        functools.partial(first_owner, n_sky),
        out_shape=[jax.ShapeDtypeStruct(picks, f32), jax.ShapeDtypeStruct((n_sky * n_exp, cap), jnp.int32), jax.ShapeDtypeStruct(tall, f32)],
        in_specs=[smem] + [vmem] * (n_sky + 1),
        compiler_params=pltpu.CompilerParams(vmem_limit_bytes=40 << 20),
    )(me, arrived, *zp)
    first = to_sources(sent)
    (sent,) = call(functools.partial(second_terms, n_sky), [terms], [slots, slots, star, star])(first, star_id, live, scale)
    arrived = to_owners(sent)
    sent, image = call(second_owner, [picks, tall])(arrived, zp_all, right, zp_index)
    second = to_sources(sent)
    sent, residual, scalars = call(
        functools.partial(third_terms, n_sky), [(n_sky * n_exp, cap + LANES), tall, (SUB, LANES)], [slots, slots, star, star]
    )(first, second, star_id, live, scale, right, image)
    arrived = to_owners(sent)
    points, left = call(last_owner, [tall, tall], [tall])(arrived, zp_all, right, image, residual, scalars)
    return points.reshape(-1)[:ZP_DEV], left.reshape(-1)[:ZP_DEV]


def solution(mesh):
    return jax.shard_map(
        body,
        mesh=mesh,
        in_specs=(
            P("sky", "exp", None, None),
            P("sky", "exp", None, None),
            P("sky", "exp", None, None),
            P("sky", "exp", None),
            P("sky", "exp", None, None),
        ),
        out_specs=(P("exp"), P("exp")),
        check_vma=False,
    )
```

```python
import functools
import math

import jax
import jax.numpy as jnp
from jax import lax
from jax.experimental import pallas as pl
from jax.experimental.pallas import tpu as pltpu
from jax.sharding import PartitionSpec as P

STAR_DEV = 4096
ZP_DEV = 12096
LANES = 128
SUB = 8
ridge = 1.0
prior = 1.0

f32 = jnp.float32
bf16 = jnp.bfloat16
i16 = jnp.int16
STAR_ROWS = STAR_DEV // LANES
ZP_ROWS = -(-ZP_DEV // (LANES * 16)) * 16
HALF_ROWS = ZP_ROWS // 2
OWNER_BLOCK = 32


def hot_rows(upper_index, lower_index, values, rows, columns):
    position = lax.broadcasted_iota(i16, (16, LANES), 0)
    high = jnp.broadcast_to(upper_index, (16, LANES)).astype(i16)
    one, zero = jnp.ones((), bf16), jnp.zeros((), bf16)
    masks = [position + jnp.int16(16 * step) == high for step in range(rows // 16)]
    upper = []
    for value in values:
        spread = jnp.broadcast_to(value, (16, LANES)).astype(bf16)
        upper.extend(jnp.where(mask, spread, zero) for mask in masks)
    low = jnp.broadcast_to(lower_index.astype(f32), (LANES, LANES)).astype(bf16).T
    lane = lax.broadcasted_iota(jnp.int32, (LANES, LANES), 1).astype(f32).astype(bf16)
    lower = [
        jnp.where(low == lane + jnp.asarray(start, bf16), one, zero)[:, :min(LANES, columns - start)]
        for start in range(0, columns, LANES)
    ]
    return jnp.concatenate(upper, 0), jnp.concatenate(lower, 1)


def halves(value):
    top = value.astype(bf16).astype(f32)
    return [top, value - top]


def sum_rows(entries, rows, columns):
    uppers, lowers = [], []
    for upper_index, lower_index, values in entries:
        parts = [part for value in values for part in halves(value)]
        upper, lower = hot_rows(upper_index, lower_index, parts, rows, columns)
        uppers.append(upper)
        lowers.append(lower)
    total = jnp.dot(jnp.concatenate(uppers, 1), jnp.concatenate(lowers, 0), preferred_element_type=f32)
    return [total[2 * n * rows:(2 * n + 1) * rows] + total[(2 * n + 1) * rows:(2 * n + 2) * rows] for n in range(len(entries[0][2]))]


def pick(table_ref, index, rows):
    high, low = index >> 7, index & 127
    found = jnp.zeros((SUB, LANES), f32)
    for row in range(rows):
        line = jnp.broadcast_to(table_ref[row:row + 1, :], (SUB, LANES))
        found = jnp.where(high == row, jnp.take_along_axis(line, low, axis=1), found)
    return found


def tiles(n_rows, cap):
    return [(g, a) for g in range(n_rows // SUB) for a in range(cap // LANES)]


def at(g, a):
    return (pl.ds(g * SUB, SUB), pl.ds(a * LANES, LANES))


def lane_row(ref, r, a):
    return ref[r:r + 1, a * LANES:(a + 1) * LANES]


def whole_sum(x):
    return jnp.sum(jnp.sum(x, axis=1, keepdims=True), axis=0, keepdims=True)


def star_sums(star_ref, value_refs, n_rows, cap, sums_refs):
    for ref in sums_refs:
        ref[...] = jnp.zeros_like(ref)

    def block(g, carry):
        stars = star_ref[pl.ds(pl.multiple_of(g * SUB, SUB), SUB), :]
        values = [ref[pl.ds(pl.multiple_of(g * SUB, SUB), SUB), :] for ref in value_refs]
        high, low = stars >> 7, stars & 127
        pairs = []
        for r in range(SUB):
            for a in range(cap // LANES):
                cut = (slice(r, r + 1), slice(a * LANES, (a + 1) * LANES))
                pairs.append((high[cut], low[cut], [value[cut] for value in values]))
        for ref, part in zip(sums_refs, sum_rows(pairs, STAR_ROWS, LANES)):
            ref[...] += part
        return carry

    lax.fori_loop(0, n_rows // SUB, block, 0)


def first_terms(n_sky, count_from, weight_from, magnitude_from, star_from, terms_ref, live_ref, scale_ref,
                count_ref, weight_ref, magnitude_ref, star_ref, moment_ref, sums_ref, mean_ref, arrival):
    n_rows, cap = weight_from.shape[2:]
    copies = [
        pltpu.make_async_copy(source, target, arrival.at[n])
        for n, (source, target) in enumerate(
            [(count_from, count_ref), (weight_from, weight_ref), (magnitude_from, magnitude_ref), (star_from, star_ref)])
    ]
    for copy in copies:
        copy.start()
    for copy in copies:
        copy.wait()
    sub = lax.broadcasted_iota(jnp.int32, (SUB, LANES), 0)
    lane = lax.broadcasted_iota(jnp.int32, (SUB, LANES), 1)
    for g in range(n_rows // SUB):
        count = jnp.zeros((SUB, LANES), jnp.int32)
        for r in range(SUB):
            count = jnp.where(sub == r, count_ref[0, 0, g * SUB + r], count)
        for a in range(cap // LANES):
            where = at(g, a)
            live = jnp.where(lane + a * LANES < count, weight_ref[(0, 0) + where], 0.0)
            live_ref[where] = live
            moment_ref[where] = live * magnitude_ref[(0, 0) + where]
    star_sums(star_ref.at[0, 0], [live_ref, moment_ref], n_rows, cap, [scale_ref, sums_ref])
    scale_ref[...] = 1.0 / (prior + scale_ref[...])
    mean_ref[...] = sums_ref[...] * scale_ref[...]
    for g in range(n_rows // SUB):
        for a in range(cap // LANES):
            where = at(g, a)
            mean = pick(mean_ref, star_ref[(0, 0) + where], STAR_ROWS)
            term = live_ref[where] * (magnitude_ref[(0, 0) + where] - mean)
            for i in range(n_sky):
                terms_ref[i * n_rows + g * SUB:i * n_rows + (g + 1) * SUB, a, :] = term


def owner_sums(zp_ref, arrived, n_rows, cap, total_ref, most=OWNER_BLOCK):
    total_ref[...] = jnp.zeros_like(total_ref)
    step = math.gcd(n_rows, most)

    def block(n, carry):
        entries = []
        for g in range(step // SUB):
            first = pl.multiple_of(n * step + g * SUB, SUB)
            index = zp_ref[pl.ds(first, SUB), :]
            row, lane = index >> 7, index & 127
            beyond = row >= HALF_ROWS
            high = jnp.where(beyond, row - HALF_ROWS, row)
            low = jnp.where(beyond, lane + LANES, lane)
            for r in range(SUB):
                for a in range(cap // LANES):
                    cut = (slice(r, r + 1), slice(a * LANES, (a + 1) * LANES))
                    entries.append((high[cut], low[cut], [arrived(first, r, a)]))
        total = sum_rows(entries, HALF_ROWS, 2 * LANES)[0]
        total_ref[0:HALF_ROWS, :] += total[:, 0:LANES]
        total_ref[HALF_ROWS:ZP_ROWS, :] += total[:, LANES:2 * LANES]
        return carry

    lax.fori_loop(0, n_rows // step, block, 0)


def send_picks(zp_ref, table_ref, out_ref, scalar):
    n_rows, cap = zp_ref.shape[2:]
    for g in range(n_rows // SUB):
        rows = slice(g * SUB, (g + 1) * SUB)

        def one(a, carry, rows=rows):
            lanes = pl.ds(pl.multiple_of(a * LANES, LANES), LANES)
            index = zp_ref[0, 0, rows, lanes]
            out_ref[rows, pl.ds(a, 1), :] = pick(table_ref, index, ZP_ROWS).reshape(SUB, 1, LANES)
            return carry

        lax.fori_loop(0, cap // LANES, one, 0, unroll=4)
    out_ref[:, cap // LANES, :] = jnp.broadcast_to(scalar, (n_rows, LANES))


def first_owner(n_sky, me_ref, arrived_ref, *refs):
    zp_refs, (sent_ref, all_ref, right_ref) = refs[:n_sky], refs[n_sky:]
    n_rows, cap = zp_refs[0].shape[2:]
    for d in range(n_sky):
        start = pl.multiple_of((me_ref[0] ^ d) * n_rows, SUB)
        all_ref[pl.ds(start, n_rows), :] = zp_refs[d][0, 0]

    def arrived(first, r, a):
        return arrived_ref[pl.ds(first + r, 1), a, :]

    owner_sums(all_ref, arrived, n_sky * n_rows, cap, right_ref, 32)
    right = right_ref[...]
    send_picks(zp_refs[0], right_ref, sent_ref, whole_sum(right * right))


def star_terms(n_sky, star_ref, live_ref, scale_ref, slot_ref, product_ref, sums_ref, mean_ref, emit):
    n_rows, cap = live_ref.shape
    for g, a in tiles(n_rows, cap):
        product_ref[at(g, a)] = live_ref[at(g, a)] * slot_ref[at(g, a)]
    star_sums(star_ref.at[0, 0], [product_ref], n_rows, cap, [sums_ref])
    mean_ref[...] = sums_ref[...] * scale_ref[...]
    along = jnp.zeros((SUB, LANES), f32)
    for g, a in tiles(n_rows, cap):
        where = at(g, a)
        mean = pick(mean_ref, star_ref[(0, 0) + where], STAR_ROWS)
        slot = slot_ref[where]
        term = live_ref[where] * (slot - mean)
        along = along + slot * term
        emit(g, a, term)
    return whole_sum(along)


def second_terms(n_sky, values_ref, star_ref, live_ref, scale_ref, terms_ref, slot_ref, product_ref, sums_ref, mean_ref):
    n_rows, cap = live_ref.shape
    for g, a in tiles(n_rows, cap):
        slot_ref[at(g, a)] = values_ref[g * SUB:(g + 1) * SUB, a, :]

    def emit(g, a, term):
        for i in range(n_sky):
            terms_ref[i * n_rows + g * SUB:i * n_rows + (g + 1) * SUB, a, :] = term

    star_terms(n_sky, star_ref, live_ref, scale_ref, slot_ref, product_ref, sums_ref, mean_ref, emit)


def second_owner(arrived_ref, all_ref, right_ref, zp_ref, sent_ref, image_ref):
    n_rows, cap = zp_ref.shape[2:]

    def arrived(first, r, a):
        return arrived_ref[pl.ds(first + r, 1), a, :]

    owner_sums(all_ref, arrived, all_ref.shape[0], cap, image_ref, 32)
    right = right_ref[...]
    image_ref[...] = image_ref[...] + ridge * right
    send_picks(zp_ref, image_ref, sent_ref, whole_sum(right * image_ref[...]))


def third_terms(n_sky, first_ref, second_ref, star_ref, live_ref, scale_ref, right_ref, image_ref,
                terms_ref, residual_ref, scalar_ref, slot_ref, product_ref, sums_ref, mean_ref):
    n_rows, cap = live_ref.shape
    extra = cap // LANES
    norm = jnp.sum(first_ref[:, extra, :], axis=0, keepdims=True)
    product = jnp.sum(second_ref[:, extra, :], axis=0, keepdims=True)
    alpha = norm / product
    scalar_ref[0:1, :] = norm
    scalar_ref[1:2, :] = alpha
    residual = right_ref[...] - alpha * image_ref[...]
    residual_ref[...] = residual
    square = whole_sum(residual * residual)
    for g, a in tiles(n_rows, cap):
        rows = slice(g * SUB, (g + 1) * SUB)
        slot_ref[at(g, a)] = first_ref[rows, a, :] - alpha * second_ref[rows, a, :]

    def emit(g, a, term):
        for i in range(n_sky):
            terms_ref[i * n_rows + g * SUB:i * n_rows + (g + 1) * SUB, a * LANES:(a + 1) * LANES] = term

    along = star_terms(n_sky, star_ref, live_ref, scale_ref, slot_ref, product_ref, sums_ref, mean_ref, emit)
    lane = lax.broadcasted_iota(jnp.int32, (1, LANES), 1)
    both = jnp.where(lane < LANES // 2, along, square * (1.0 / n_sky))
    terms_ref[:, cap:cap + LANES] = jnp.broadcast_to(both, (n_sky * n_rows, LANES))


def last_owner(arrived_ref, all_ref, right_ref, image_ref, residual_ref, scalar_ref, points_ref, left_ref, total_ref):
    cap = all_ref.shape[1]

    def arrived(first, r, a):
        return arrived_ref[pl.ds(first, SUB), a * LANES:(a + 1) * LANES][r:r + 1]

    owner_sums(all_ref, arrived, all_ref.shape[0], cap, total_ref)
    sums = jnp.sum(arrived_ref[:, cap:cap + LANES], axis=0, keepdims=True)
    norm_next = sums[:, LANES // 2:LANES // 2 + 1]
    product = sums[:, 0:1] + ridge * norm_next
    norm, alpha = scalar_ref[0:1, 0:1], scalar_ref[1:2, 0:1]
    ratio = norm_next / norm
    step = norm_next / (product - ratio * norm_next / alpha)
    right, residual = right_ref[...], residual_ref[...]
    direction = residual + ratio * right
    along = (total_ref[...] + ridge * residual) + ratio * image_ref[...]
    points_ref[...] = alpha * right + step * direction
    left_ref[...] = residual - step * along


def call(kernel, shapes, scratch=(), flops=2_000_000, **more):
    return pl.pallas_call(
        kernel,
        out_shape=[jax.ShapeDtypeStruct(shape, f32) for shape in shapes],
        scratch_shapes=[pltpu.VMEM(shape, f32) for shape in scratch],
        compiler_params=pltpu.CompilerParams(vmem_limit_bytes=40 << 20),
        cost_estimate=pl.CostEstimate(flops=flops * 1000, bytes_accessed=1 << 20, transcendentals=0),
        **more,
    )


def body(obs_weight, magnitude, star_id, peer_count, zp_index):
    n_sky, n_exp = lax.axis_size("sky"), lax.axis_size("exp")
    cap = obs_weight.shape[3]
    tall, star, slots = (ZP_ROWS, LANES), (STAR_ROWS, LANES), (n_exp, cap)
    terms = (n_sky * n_exp, cap // LANES, LANES)
    picks = (n_exp, 2 * SUB, LANES)
    vmem = pl.BlockSpec(memory_space=pltpu.VMEM)
    smem = pl.BlockSpec(memory_space=pltpu.SMEM)
    me = jnp.reshape(lax.axis_index("sky"), (1,)).astype(jnp.int32)

    def to_owners(x):
        return lax.all_to_all(x, ("sky", "exp"), split_axis=0, concat_axis=0, tiled=True)

    def to_sources(x):
        return lax.all_to_all(x, "exp", split_axis=0, concat_axis=0, tiled=True)

    zp = [zp_index] + [lax.ppermute(zp_index, "sky", [(i, i ^ d) for i in range(n_sky)]) for d in range(1, n_sky)]
    anywhere = pl.BlockSpec(memory_space=pl.ANY)
    whole = (1, 1, n_exp, cap)
    sent, live, scale = pl.pallas_call(
        functools.partial(first_terms, n_sky),
        out_shape=[jax.ShapeDtypeStruct(shape, f32) for shape in (terms, slots, star)],
        in_specs=[anywhere] * 4,
        scratch_shapes=[pltpu.SMEM((1, 1, n_exp), jnp.int32), pltpu.VMEM(whole, f32), pltpu.VMEM(whole, f32), pltpu.VMEM(whole, jnp.int32),
                        pltpu.VMEM(slots, f32), pltpu.VMEM(star, f32), pltpu.VMEM(star, f32), pltpu.SemaphoreType.DMA((4,))],
        compiler_params=pltpu.CompilerParams(vmem_limit_bytes=58 << 20),
        cost_estimate=pl.CostEstimate(flops=2_000_000_000, bytes_accessed=1 << 20, transcendentals=0),
    )(peer_count, obs_weight, magnitude, star_id)
    arrived = to_owners(sent)
    sent, zp_all, right = pl.pallas_call(
        functools.partial(first_owner, n_sky),
        out_shape=[jax.ShapeDtypeStruct(picks, f32), jax.ShapeDtypeStruct((n_sky * n_exp, cap), jnp.int32), jax.ShapeDtypeStruct(tall, f32)],
        in_specs=[smem] + [vmem] * (n_sky + 1),
        compiler_params=pltpu.CompilerParams(vmem_limit_bytes=40 << 20),
    )(me, arrived, *zp)
    first = to_sources(sent)
    (sent,) = call(functools.partial(second_terms, n_sky), [terms], [slots, slots, star, star])(first, star_id, live, scale)
    arrived = to_owners(sent)
    sent, image = call(second_owner, [picks, tall])(arrived, zp_all, right, zp_index)
    second = to_sources(sent)
    sent, residual, scalars = call(
        functools.partial(third_terms, n_sky), [(n_sky * n_exp, cap + LANES), tall, (SUB, LANES)], [slots, slots, star, star]
    )(first, second, star_id, live, scale, right, image)
    arrived = to_owners(sent)
    points, left = call(last_owner, [tall, tall], [tall])(arrived, zp_all, right, image, residual, scalars)
    return points.reshape(-1)[:ZP_DEV], left.reshape(-1)[:ZP_DEV]


def solution(mesh):
    return jax.shard_map(
        body,
        mesh=mesh,
        in_specs=(
            P("sky", "exp", None, None),
            P("sky", "exp", None, None),
            P("sky", "exp", None, None),
            P("sky", "exp", None),
            P("sky", "exp", None, None),
        ),
        out_specs=(P("exp"), P("exp")),
        check_vma=False,
    )
```

```python
import functools
import math

import jax
import jax.numpy as jnp
from jax import lax
from jax.experimental import pallas as pl
from jax.experimental.pallas import tpu as pltpu
from jax.sharding import PartitionSpec as P

STAR_DEV = 4096
ZP_DEV = 12096
LANES = 128
SUB = 8
ridge = 1.0
prior = 1.0

f32 = jnp.float32
bf16 = jnp.bfloat16
i16 = jnp.int16
STAR_ROWS = STAR_DEV // LANES
ZP_ROWS = -(-ZP_DEV // (LANES * 16)) * 16
HALF_ROWS = ZP_ROWS // 2
OWNER_BLOCK = 32


def hot_rows(upper_index, lower_index, values, rows, columns):
    position = lax.broadcasted_iota(i16, (16, LANES), 0)
    high = jnp.broadcast_to(upper_index, (16, LANES)).astype(i16)
    one, zero = jnp.ones((), bf16), jnp.zeros((), bf16)
    masks = [position + jnp.int16(16 * step) == high for step in range(rows // 16)]
    upper = []
    for value in values:
        spread = jnp.broadcast_to(value, (16, LANES)).astype(bf16)
        upper.extend(jnp.where(mask, spread, zero) for mask in masks)
    low = jnp.broadcast_to(lower_index.astype(f32), (LANES, LANES)).astype(bf16).T
    lane = lax.broadcasted_iota(jnp.int32, (LANES, LANES), 1).astype(f32).astype(bf16)
    lower = [
        jnp.where(low == lane + jnp.asarray(start, bf16), one, zero)[:, :min(LANES, columns - start)]
        for start in range(0, columns, LANES)
    ]
    return jnp.concatenate(upper, 0), jnp.concatenate(lower, 1)


def halves(value):
    top = value.astype(bf16).astype(f32)
    return [top, value - top]


def sum_rows(entries, rows, columns):
    uppers, lowers = [], []
    for upper_index, lower_index, values in entries:
        parts = [part for value in values for part in halves(value)]
        upper, lower = hot_rows(upper_index, lower_index, parts, rows, columns)
        uppers.append(upper)
        lowers.append(lower)
    total = jnp.dot(jnp.concatenate(uppers, 1), jnp.concatenate(lowers, 0), preferred_element_type=f32)
    return [total[2 * n * rows:(2 * n + 1) * rows] + total[(2 * n + 1) * rows:(2 * n + 2) * rows] for n in range(len(entries[0][2]))]


def pick(table_ref, index, rows):
    high, low = index >> 7, index & 127
    found = jnp.zeros((SUB, LANES), f32)
    for row in range(rows):
        line = jnp.broadcast_to(table_ref[row:row + 1, :], (SUB, LANES))
        found = jnp.where(high == row, jnp.take_along_axis(line, low, axis=1), found)
    return found


def tiles(n_rows, cap):
    return [(g, a) for g in range(n_rows // SUB) for a in range(cap // LANES)]


def at(g, a):
    return (pl.ds(g * SUB, SUB), pl.ds(a * LANES, LANES))


def lane_row(ref, r, a):
    return ref[r:r + 1, a * LANES:(a + 1) * LANES]


def whole_sum(x):
    return jnp.sum(jnp.sum(x, axis=1, keepdims=True), axis=0, keepdims=True)


def star_sums(star_ref, value_refs, n_rows, cap, sums_refs):
    for ref in sums_refs:
        ref[...] = jnp.zeros_like(ref)

    def block(g, carry):
        stars = star_ref[pl.ds(pl.multiple_of(g * SUB, SUB), SUB), :]
        values = [ref[pl.ds(pl.multiple_of(g * SUB, SUB), SUB), :] for ref in value_refs]
        high, low = stars >> 7, stars & 127
        pairs = []
        for r in range(SUB):
            for a in range(cap // LANES):
                cut = (slice(r, r + 1), slice(a * LANES, (a + 1) * LANES))
                pairs.append((high[cut], low[cut], [value[cut] for value in values]))
        for ref, part in zip(sums_refs, sum_rows(pairs, STAR_ROWS, LANES)):
            ref[...] += part
        return carry

    lax.fori_loop(0, n_rows // SUB, block, 0)


def first_terms(n_sky, count_from, weight_from, magnitude_from, star_from, terms_ref, live_ref, scale_ref,
                count_ref, weight_ref, magnitude_ref, star_ref, moment_ref, sums_ref, mean_ref, arrival):
    n_rows, cap = weight_from.shape[2:]
    copies = [
        pltpu.make_async_copy(source, target, arrival.at[n])
        for n, (source, target) in enumerate(
            [(count_from, count_ref), (weight_from, weight_ref), (magnitude_from, magnitude_ref), (star_from, star_ref)])
    ]
    for copy in copies:
        copy.start()
    for copy in copies:
        copy.wait()
    sub = lax.broadcasted_iota(jnp.int32, (SUB, LANES), 0)
    lane = lax.broadcasted_iota(jnp.int32, (SUB, LANES), 1)
    for g in range(n_rows // SUB):
        count = jnp.zeros((SUB, LANES), jnp.int32)
        for r in range(SUB):
            count = jnp.where(sub == r, count_ref[0, 0, g * SUB + r], count)
        for a in range(cap // LANES):
            where = at(g, a)
            live = jnp.where(lane + a * LANES < count, weight_ref[(0, 0) + where], 0.0)
            live_ref[where] = live
            moment_ref[where] = live * magnitude_ref[(0, 0) + where]
    star_sums(star_ref.at[0, 0], [live_ref, moment_ref], n_rows, cap, [scale_ref, sums_ref])
    scale_ref[...] = 1.0 / (prior + scale_ref[...])
    mean_ref[...] = sums_ref[...] * scale_ref[...]
    for g in range(n_rows // SUB):
        for a in range(cap // LANES):
            where = at(g, a)
            mean = pick(mean_ref, star_ref[(0, 0) + where], STAR_ROWS)
            term = live_ref[where] * (magnitude_ref[(0, 0) + where] - mean)
            for i in range(n_sky):
                terms_ref[i * n_rows + g * SUB:i * n_rows + (g + 1) * SUB, a, :] = term


def owner_sums(zp_ref, arrived, n_rows, cap, total_ref, most=OWNER_BLOCK):
    total_ref[...] = jnp.zeros_like(total_ref)
    step = math.gcd(n_rows, most)

    def block(n, carry):
        entries = []
        for g in range(step // SUB):
            first = pl.multiple_of(n * step + g * SUB, SUB)
            index = zp_ref[pl.ds(first, SUB), :]
            row, lane = index >> 7, index & 127
            beyond = row >= HALF_ROWS
            high = jnp.where(beyond, row - HALF_ROWS, row)
            low = jnp.where(beyond, lane + LANES, lane)
            for r in range(SUB):
                for a in range(cap // LANES):
                    cut = (slice(r, r + 1), slice(a * LANES, (a + 1) * LANES))
                    entries.append((high[cut], low[cut], [arrived(first, r, a)]))
        total = sum_rows(entries, HALF_ROWS, 2 * LANES)[0]
        total_ref[0:HALF_ROWS, :] += total[:, 0:LANES]
        total_ref[HALF_ROWS:ZP_ROWS, :] += total[:, LANES:2 * LANES]
        return carry

    lax.fori_loop(0, n_rows // step, block, 0)


def send_picks(zp_ref, table_ref, out_ref, extra=0):
    n_rows, cap = zp_ref.shape[2:]
    block = cap // LANES + extra
    for g in range(n_rows // SUB):
        rows = slice(g * SUB, (g + 1) * SUB)

        def one(a, carry, rows=rows):
            lanes = pl.ds(pl.multiple_of(a * LANES, LANES), LANES)
            index = zp_ref[0, 0, rows, lanes]
            out_ref[pl.ds(rows.start * block + a, SUB, stride=block), :] = pick(table_ref, index, ZP_ROWS)
            return carry

        lax.fori_loop(0, cap // LANES, one, 0, unroll=4)


def first_owner(n_sky, me_ref, arrived_ref, *refs):
    zp_refs, (sent_ref, all_ref, right_ref) = refs[:n_sky], refs[n_sky:]
    n_rows, cap = zp_refs[0].shape[2:]
    for d in range(n_sky):
        start = pl.multiple_of((me_ref[0] ^ d) * n_rows, SUB)
        all_ref[pl.ds(start, n_rows), :] = zp_refs[d][0, 0]

    def arrived(first, r, a):
        return arrived_ref[pl.ds(first + r, 1), a, :]

    owner_sums(all_ref, arrived, n_sky * n_rows, cap, right_ref, 32)
    send_picks(zp_refs[0], right_ref, sent_ref)


def star_terms(n_sky, star_ref, live_ref, scale_ref, slot_ref, product_ref, sums_ref, mean_ref, emit):
    n_rows, cap = live_ref.shape
    for g, a in tiles(n_rows, cap):
        product_ref[at(g, a)] = live_ref[at(g, a)] * slot_ref[at(g, a)]
    star_sums(star_ref.at[0, 0], [product_ref], n_rows, cap, [sums_ref])
    mean_ref[...] = sums_ref[...] * scale_ref[...]
    along = jnp.zeros((SUB, LANES), f32)
    for g, a in tiles(n_rows, cap):
        where = at(g, a)
        mean = pick(mean_ref, star_ref[(0, 0) + where], STAR_ROWS)
        slot = slot_ref[where]
        term = live_ref[where] * (slot - mean)
        along = along + slot * term
        emit(g, a, term)
    return whole_sum(along)


def second_terms(n_sky, values_ref, star_ref, live_ref, scale_ref, terms_ref, slot_ref, product_ref, sums_ref, mean_ref):
    n_rows, cap = live_ref.shape
    for g, a in tiles(n_rows, cap):
        slot_ref[at(g, a)] = values_ref[g * SUB:(g + 1) * SUB, a, :]

    def emit(g, a, term):
        for i in range(n_sky):
            terms_ref[i * n_rows + g * SUB:i * n_rows + (g + 1) * SUB, a, :] = term

    star_terms(n_sky, star_ref, live_ref, scale_ref, slot_ref, product_ref, sums_ref, mean_ref, emit)


def second_owner(arrived_ref, all_ref, right_ref, zp_ref, sent_ref, image_ref):
    n_rows, cap = zp_ref.shape[2:]

    def arrived(first, r, a):
        return arrived_ref[pl.ds(first + r, 1), a, :]

    owner_sums(all_ref, arrived, all_ref.shape[0], cap, image_ref, 32)
    right = right_ref[...]
    image_ref[...] = image_ref[...] + ridge * right
    send_picks(zp_ref, image_ref, sent_ref, 1)
    lane = lax.broadcasted_iota(jnp.int32, (1, LANES), 1)
    both = jnp.where(lane < LANES // 2, whole_sum(right * right), whole_sum(right * image_ref[...]))
    block = cap // LANES + 1
    sent_ref[pl.ds(block - 1, n_rows, stride=block), :] = jnp.broadcast_to(both, (n_rows, LANES))


def third_terms(n_sky, first_ref, second_ref, star_ref, live_ref, scale_ref, right_ref, image_ref,
                terms_ref, residual_ref, scalar_ref, slot_ref, product_ref, sums_ref, mean_ref):
    n_rows, cap = live_ref.shape
    extra = cap // LANES
    sums = jnp.sum(second_ref[:, cap:cap + LANES], axis=0, keepdims=True)
    norm = jnp.broadcast_to(sums[:, 0:1], (1, LANES))
    product = jnp.broadcast_to(sums[:, LANES // 2:LANES // 2 + 1], (1, LANES))
    alpha = norm / product
    scalar_ref[0:1, :] = norm
    scalar_ref[1:2, :] = alpha
    residual = right_ref[...] - alpha * image_ref[...]
    residual_ref[...] = residual
    square = whole_sum(residual * residual)
    for g, a in tiles(n_rows, cap):
        rows = slice(g * SUB, (g + 1) * SUB)
        slot_ref[at(g, a)] = first_ref[rows, a, :] - alpha * second_ref[at(g, a)]

    def emit(g, a, term):
        for i in range(n_sky):
            terms_ref[pl.ds((i * n_rows + g * SUB) * (extra + 1) + a, SUB, stride=extra + 1), :] = term

    along = star_terms(n_sky, star_ref, live_ref, scale_ref, slot_ref, product_ref, sums_ref, mean_ref, emit)
    lane = lax.broadcasted_iota(jnp.int32, (1, LANES), 1)
    both = jnp.where(lane < LANES // 2, along, square * (1.0 / n_sky))
    terms_ref[pl.ds(extra, n_sky * n_rows, stride=extra + 1), :] = jnp.broadcast_to(both, (n_sky * n_rows, LANES))


def last_owner(arrived_ref, all_ref, right_ref, image_ref, residual_ref, scalar_ref, points_ref, left_ref, total_ref):
    cap = all_ref.shape[1]

    def arrived(first, r, a):
        return arrived_ref[pl.ds(first, SUB), a * LANES:(a + 1) * LANES][r:r + 1]

    owner_sums(all_ref, arrived, all_ref.shape[0], cap, total_ref)
    sums = jnp.sum(arrived_ref[:, cap:cap + LANES], axis=0, keepdims=True)
    norm_next = sums[:, LANES // 2:LANES // 2 + 1]
    product = sums[:, 0:1] + ridge * norm_next
    norm, alpha = scalar_ref[0:1, 0:1], scalar_ref[1:2, 0:1]
    ratio = norm_next / norm
    step = norm_next / (product - ratio * norm_next / alpha)
    right, residual = right_ref[...], residual_ref[...]
    direction = residual + ratio * right
    along = (total_ref[...] + ridge * residual) + ratio * image_ref[...]
    points_ref[...] = alpha * right + step * direction
    left_ref[...] = residual - step * along


def call(kernel, shapes, scratch=(), flops=2_000_000, **more):
    return pl.pallas_call(
        kernel,
        out_shape=[jax.ShapeDtypeStruct(shape, f32) for shape in shapes],
        scratch_shapes=[pltpu.VMEM(shape, f32) for shape in scratch],
        compiler_params=pltpu.CompilerParams(vmem_limit_bytes=40 << 20),
        cost_estimate=pl.CostEstimate(flops=flops * 1000, bytes_accessed=1 << 20, transcendentals=0),
        **more,
    )


def body(obs_weight, magnitude, star_id, peer_count, zp_index):
    n_sky, n_exp = lax.axis_size("sky"), lax.axis_size("exp")
    cap = obs_weight.shape[3]
    tall, star, slots = (ZP_ROWS, LANES), (STAR_ROWS, LANES), (n_exp, cap)
    terms = (n_sky * n_exp, cap // LANES, LANES)
    picks = (n_exp * (cap // LANES + 1), LANES)
    vmem = pl.BlockSpec(memory_space=pltpu.VMEM)
    smem = pl.BlockSpec(memory_space=pltpu.SMEM)
    me = jnp.reshape(lax.axis_index("sky"), (1,)).astype(jnp.int32)

    def to_owners(x):
        return lax.all_to_all(x, ("sky", "exp"), split_axis=0, concat_axis=0, tiled=True)

    def to_sources(x):
        return lax.all_to_all(x, "exp", split_axis=0, concat_axis=0, tiled=True)

    zp = [zp_index] + [lax.ppermute(zp_index, "sky", [(i, i ^ d) for i in range(n_sky)]) for d in range(1, n_sky)]
    anywhere = pl.BlockSpec(memory_space=pl.ANY)
    whole = (1, 1, n_exp, cap)
    sent, live, scale = pl.pallas_call(
        functools.partial(first_terms, n_sky),
        out_shape=[jax.ShapeDtypeStruct(shape, f32) for shape in (terms, slots, star)],
        in_specs=[anywhere] * 4,
        scratch_shapes=[pltpu.SMEM((1, 1, n_exp), jnp.int32), pltpu.VMEM(whole, f32), pltpu.VMEM(whole, f32), pltpu.VMEM(whole, jnp.int32),
                        pltpu.VMEM(slots, f32), pltpu.VMEM(star, f32), pltpu.VMEM(star, f32), pltpu.SemaphoreType.DMA((4,))],
        compiler_params=pltpu.CompilerParams(vmem_limit_bytes=58 << 20),
        cost_estimate=pl.CostEstimate(flops=2_000_000_000, bytes_accessed=1 << 20, transcendentals=0),
    )(peer_count, obs_weight, magnitude, star_id)
    arrived = to_owners(sent)
    sent, zp_all, right = pl.pallas_call(
        functools.partial(first_owner, n_sky),
        out_shape=[jax.ShapeDtypeStruct((n_exp * (cap // LANES), LANES), f32), jax.ShapeDtypeStruct((n_sky * n_exp, cap), jnp.int32), jax.ShapeDtypeStruct(tall, f32)],
        in_specs=[smem] + [vmem] * (n_sky + 1),
        compiler_params=pltpu.CompilerParams(vmem_limit_bytes=40 << 20),
    )(me, arrived, *zp)
    first = to_sources(sent.reshape(n_exp, cap // LANES, LANES))
    (sent,) = call(functools.partial(second_terms, n_sky), [terms], [slots, slots, star, star])(first, star_id, live, scale)
    arrived = to_owners(sent)
    sent, image = call(second_owner, [picks, tall])(arrived, zp_all, right, zp_index)
    second = to_sources(sent.reshape(n_exp, cap + LANES))
    sent, residual, scalars = call(
        functools.partial(third_terms, n_sky), [(n_sky * n_exp * (cap // LANES + 1), LANES), tall, (SUB, LANES)], [slots, slots, star, star]
    )(first, second, star_id, live, scale, right, image)
    arrived = to_owners(sent.reshape(n_sky * n_exp, cap + LANES))
    points, left = call(last_owner, [tall, tall], [tall])(arrived, zp_all, right, image, residual, scalars)
    return points.reshape(-1)[:ZP_DEV], left.reshape(-1)[:ZP_DEV]


def solution(mesh):
    return jax.shard_map(
        body,
        mesh=mesh,
        in_specs=(
            P("sky", "exp", None, None),
            P("sky", "exp", None, None),
            P("sky", "exp", None, None),
            P("sky", "exp", None),
            P("sky", "exp", None, None),
        ),
        out_specs=(P("exp"), P("exp")),
        check_vma=False,
    )
```

```python
import functools
import math

import jax
import jax.numpy as jnp
from jax import lax
from jax.experimental import pallas as pl
from jax.experimental.pallas import tpu as pltpu
from jax.sharding import PartitionSpec as P

STAR_DEV = 4096
ZP_DEV = 12096
LANES = 128
SUB = 8
ridge = 1.0
prior = 1.0

f32 = jnp.float32
bf16 = jnp.bfloat16
i16 = jnp.int16
STAR_ROWS = STAR_DEV // LANES
ZP_ROWS = -(-ZP_DEV // (LANES * 16)) * 16
HALF_ROWS = ZP_ROWS // 2
OWNER_BLOCK = 32


def hot_rows(upper_index, lower_index, values, rows, columns):
    position = lax.broadcasted_iota(i16, (16, LANES), 0)
    high = jnp.broadcast_to(upper_index, (16, LANES)).astype(i16)
    one, zero = jnp.ones((), bf16), jnp.zeros((), bf16)
    masks = [position + jnp.int16(16 * step) == high for step in range(rows // 16)]
    upper = []
    for value in values:
        spread = jnp.broadcast_to(value, (16, LANES)).astype(bf16)
        upper.extend(jnp.where(mask, spread, zero) for mask in masks)
    low = jnp.broadcast_to(lower_index.astype(f32), (LANES, LANES)).astype(bf16).T
    lane = lax.broadcasted_iota(jnp.int32, (LANES, LANES), 1).astype(f32).astype(bf16)
    lower = [
        jnp.where(low == lane + jnp.asarray(start, bf16), one, zero)[:, :min(LANES, columns - start)]
        for start in range(0, columns, LANES)
    ]
    return jnp.concatenate(upper, 0), jnp.concatenate(lower, 1)


def halves(value):
    top = value.astype(bf16).astype(f32)
    return [top, value - top]


def sum_rows(entries, rows, columns):
    uppers, lowers = [], []
    for upper_index, lower_index, values in entries:
        parts = [part for value in values for part in halves(value)]
        upper, lower = hot_rows(upper_index, lower_index, parts, rows, columns)
        uppers.append(upper)
        lowers.append(lower)
    total = jnp.dot(jnp.concatenate(uppers, 1), jnp.concatenate(lowers, 0), preferred_element_type=f32)
    return [total[2 * n * rows:(2 * n + 1) * rows] + total[(2 * n + 1) * rows:(2 * n + 2) * rows] for n in range(len(entries[0][2]))]


def pick(table_ref, index, rows):
    high, low = index >> 7, index & 127
    found = jnp.zeros((SUB, LANES), f32)
    for row in range(rows):
        line = jnp.broadcast_to(table_ref[row:row + 1, :], (SUB, LANES))
        found = jnp.where(high == row, jnp.take_along_axis(line, low, axis=1), found)
    return found


def tiles(n_rows, cap):
    return [(g, a) for g in range(n_rows // SUB) for a in range(cap // LANES)]


def at(g, a):
    return (pl.ds(g * SUB, SUB), pl.ds(a * LANES, LANES))


def lane_row(ref, r, a):
    return ref[r:r + 1, a * LANES:(a + 1) * LANES]


def whole_sum(x):
    return jnp.sum(jnp.sum(x, axis=1, keepdims=True), axis=0, keepdims=True)


def star_sums(star_ref, value_refs, n_rows, cap, sums_refs):
    for ref in sums_refs:
        ref[...] = jnp.zeros_like(ref)

    def block(g, carry):
        stars = star_ref[pl.ds(pl.multiple_of(g * SUB, SUB), SUB), :]
        values = [ref[pl.ds(pl.multiple_of(g * SUB, SUB), SUB), :] for ref in value_refs]
        high, low = stars >> 7, stars & 127
        pairs = []
        for r in range(SUB):
            for a in range(cap // LANES):
                cut = (slice(r, r + 1), slice(a * LANES, (a + 1) * LANES))
                pairs.append((high[cut], low[cut], [value[cut] for value in values]))
        for ref, part in zip(sums_refs, sum_rows(pairs, STAR_ROWS, LANES)):
            ref[...] += part
        return carry

    lax.fori_loop(0, n_rows // SUB, block, 0)


def first_terms(n_sky, count_from, weight_from, magnitude_from, star_from, terms_ref, live_ref, scale_ref,
                count_ref, weight_ref, magnitude_ref, star_ref, moment_ref, sums_ref, mean_ref, arrival):
    n_rows, cap = weight_from.shape[2:]
    copies = [
        pltpu.make_async_copy(source, target, arrival.at[n])
        for n, (source, target) in enumerate(
            [(count_from, count_ref), (weight_from, weight_ref), (magnitude_from, magnitude_ref), (star_from, star_ref)])
    ]
    for copy in copies:
        copy.start()
    for copy in copies:
        copy.wait()
    sub = lax.broadcasted_iota(jnp.int32, (SUB, LANES), 0)
    lane = lax.broadcasted_iota(jnp.int32, (SUB, LANES), 1)
    for g in range(n_rows // SUB):
        count = jnp.zeros((SUB, LANES), jnp.int32)
        for r in range(SUB):
            count = jnp.where(sub == r, count_ref[0, 0, g * SUB + r], count)
        for a in range(cap // LANES):
            where = at(g, a)
            live = jnp.where(lane + a * LANES < count, weight_ref[(0, 0) + where], 0.0)
            live_ref[where] = live
            moment_ref[where] = live * magnitude_ref[(0, 0) + where]
    star_sums(star_ref.at[0, 0], [live_ref, moment_ref], n_rows, cap, [scale_ref, sums_ref])
    scale_ref[...] = 1.0 / (prior + scale_ref[...])
    mean_ref[...] = sums_ref[...] * scale_ref[...]
    for g in range(n_rows // SUB):
        for a in range(cap // LANES):
            where = at(g, a)
            mean = pick(mean_ref, star_ref[(0, 0) + where], STAR_ROWS)
            term = live_ref[where] * (magnitude_ref[(0, 0) + where] - mean)
            for i in range(n_sky):
                terms_ref[i * n_rows + g * SUB:i * n_rows + (g + 1) * SUB, a, :] = term


def owner_sums(zp_ref, arrived, n_rows, cap, total_ref, most=OWNER_BLOCK):
    total_ref[...] = jnp.zeros_like(total_ref)
    step = math.gcd(n_rows, most)

    def block(n, carry):
        entries = []
        for g in range(step // SUB):
            first = pl.multiple_of(n * step + g * SUB, SUB)
            index = zp_ref[pl.ds(first, SUB), :]
            row, lane = index >> 7, index & 127
            beyond = row >= HALF_ROWS
            high = jnp.where(beyond, row - HALF_ROWS, row)
            low = jnp.where(beyond, lane + LANES, lane)
            for r in range(SUB):
                for a in range(cap // LANES):
                    cut = (slice(r, r + 1), slice(a * LANES, (a + 1) * LANES))
                    entries.append((high[cut], low[cut], [arrived(first, r, a)]))
        total = sum_rows(entries, HALF_ROWS, 2 * LANES)[0]
        total_ref[0:HALF_ROWS, :] += total[:, 0:LANES]
        total_ref[HALF_ROWS:ZP_ROWS, :] += total[:, LANES:2 * LANES]
        return carry

    lax.fori_loop(0, n_rows // step, block, 0)


def send_picks(zp_ref, table_ref, out_ref, extra=0):
    n_rows, cap = zp_ref.shape[2:]
    block = cap // LANES + extra
    for g in range(n_rows // SUB):
        rows = slice(g * SUB, (g + 1) * SUB)

        def one(a, carry, rows=rows):
            lanes = pl.ds(pl.multiple_of(a * LANES, LANES), LANES)
            index = zp_ref[0, 0, rows, lanes]
            out_ref[pl.ds(rows.start * block + a, SUB, stride=block), :] = pick(table_ref, index, ZP_ROWS)
            return carry

        lax.fori_loop(0, cap // LANES, one, 0, unroll=4)


def own_owner(me_ref, arrived_ref, zp_ref, part_ref):
    n_rows, cap = zp_ref.shape[2:]
    base = me_ref[0] * n_rows

    def arrived(first, r, a):
        return arrived_ref[pl.ds(base + first + r, 1), a, :]

    owner_sums(zp_ref.at[0, 0], arrived, n_rows, cap, part_ref)


def first_owner(n_sky, me_ref, arrived_ref, part_ref, *refs):
    zp_refs, (sent_ref, all_ref, right_ref, parts_ref, one_ref) = refs[:n_sky], refs[n_sky:]
    n_rows, cap = zp_refs[0].shape[2:]
    parts_ref[pl.ds(pl.multiple_of(me_ref[0] * ZP_ROWS, SUB), ZP_ROWS), :] = part_ref[...]
    for d in range(n_sky):
        group = me_ref[0] ^ d
        base = pl.multiple_of(group * n_rows, SUB)
        all_ref[pl.ds(base, n_rows), :] = zp_refs[d][0, 0]
        if d:

            def arrived(first, r, a, base=base):
                return arrived_ref[pl.ds(base + first + r, 1), a, :]

            owner_sums(zp_refs[d].at[0, 0], arrived, n_rows, cap, one_ref)
            parts_ref[pl.ds(pl.multiple_of(group * ZP_ROWS, SUB), ZP_ROWS), :] = one_ref[...]
    right = parts_ref[0:ZP_ROWS, :]
    for n in range(1, n_sky):
        right = right + parts_ref[n * ZP_ROWS:(n + 1) * ZP_ROWS, :]
    right_ref[...] = right
    send_picks(zp_refs[0], right_ref, sent_ref)


def star_terms(n_sky, star_ref, live_ref, scale_ref, slot_ref, product_ref, sums_ref, mean_ref, emit):
    n_rows, cap = live_ref.shape
    for g, a in tiles(n_rows, cap):
        product_ref[at(g, a)] = live_ref[at(g, a)] * slot_ref[at(g, a)]
    star_sums(star_ref.at[0, 0], [product_ref], n_rows, cap, [sums_ref])
    mean_ref[...] = sums_ref[...] * scale_ref[...]
    along = jnp.zeros((SUB, LANES), f32)
    for g, a in tiles(n_rows, cap):
        where = at(g, a)
        mean = pick(mean_ref, star_ref[(0, 0) + where], STAR_ROWS)
        slot = slot_ref[where]
        term = live_ref[where] * (slot - mean)
        along = along + slot * term
        emit(g, a, term)
    return whole_sum(along)


def second_terms(n_sky, values_ref, star_ref, live_ref, scale_ref, terms_ref, slot_ref, product_ref, sums_ref, mean_ref):
    n_rows, cap = live_ref.shape
    for g, a in tiles(n_rows, cap):
        slot_ref[at(g, a)] = values_ref[g * SUB:(g + 1) * SUB, a, :]

    def emit(g, a, term):
        for i in range(n_sky):
            terms_ref[i * n_rows + g * SUB:i * n_rows + (g + 1) * SUB, a, :] = term

    star_terms(n_sky, star_ref, live_ref, scale_ref, slot_ref, product_ref, sums_ref, mean_ref, emit)


def second_owner(arrived_ref, all_ref, right_ref, zp_ref, sent_ref, image_ref):
    n_rows, cap = zp_ref.shape[2:]

    def arrived(first, r, a):
        return arrived_ref[pl.ds(first + r, 1), a, :]

    owner_sums(all_ref, arrived, all_ref.shape[0], cap, image_ref, 32)
    right = right_ref[...]
    image_ref[...] = image_ref[...] + ridge * right
    send_picks(zp_ref, image_ref, sent_ref, 1)
    lane = lax.broadcasted_iota(jnp.int32, (1, LANES), 1)
    both = jnp.where(lane < LANES // 2, whole_sum(right * right), whole_sum(right * image_ref[...]))
    block = cap // LANES + 1
    sent_ref[pl.ds(block - 1, n_rows, stride=block), :] = jnp.broadcast_to(both, (n_rows, LANES))


def third_terms(n_sky, first_ref, second_ref, star_ref, live_ref, scale_ref, right_ref, image_ref,
                terms_ref, residual_ref, scalar_ref, slot_ref, product_ref, sums_ref, mean_ref):
    n_rows, cap = live_ref.shape
    extra = cap // LANES
    sums = jnp.sum(second_ref[:, cap:cap + LANES], axis=0, keepdims=True)
    norm = jnp.broadcast_to(sums[:, 0:1], (1, LANES))
    product = jnp.broadcast_to(sums[:, LANES // 2:LANES // 2 + 1], (1, LANES))
    alpha = norm / product
    scalar_ref[0:1, :] = norm
    scalar_ref[1:2, :] = alpha
    residual = right_ref[...] - alpha * image_ref[...]
    residual_ref[...] = residual
    square = whole_sum(residual * residual)
    for g, a in tiles(n_rows, cap):
        rows = slice(g * SUB, (g + 1) * SUB)
        slot_ref[at(g, a)] = first_ref[rows, a, :] - alpha * second_ref[at(g, a)]

    def emit(g, a, term):
        for i in range(n_sky):
            terms_ref[pl.ds((i * n_rows + g * SUB) * (extra + 1) + a, SUB, stride=extra + 1), :] = term

    along = star_terms(n_sky, star_ref, live_ref, scale_ref, slot_ref, product_ref, sums_ref, mean_ref, emit)
    lane = lax.broadcasted_iota(jnp.int32, (1, LANES), 1)
    both = jnp.where(lane < LANES // 2, along, square * (1.0 / n_sky))
    terms_ref[pl.ds(extra, n_sky * n_rows, stride=extra + 1), :] = jnp.broadcast_to(both, (n_sky * n_rows, LANES))


def last_owner(arrived_ref, all_ref, right_ref, image_ref, residual_ref, scalar_ref, points_ref, left_ref, total_ref):
    cap = all_ref.shape[1]

    def arrived(first, r, a):
        return arrived_ref[pl.ds(first, SUB), a * LANES:(a + 1) * LANES][r:r + 1]

    owner_sums(all_ref, arrived, all_ref.shape[0], cap, total_ref)
    sums = jnp.sum(arrived_ref[:, cap:cap + LANES], axis=0, keepdims=True)
    norm_next = sums[:, LANES // 2:LANES // 2 + 1]
    product = sums[:, 0:1] + ridge * norm_next
    norm, alpha = scalar_ref[0:1, 0:1], scalar_ref[1:2, 0:1]
    ratio = norm_next / norm
    step = norm_next / (product - ratio * norm_next / alpha)
    right, residual = right_ref[...], residual_ref[...]
    direction = residual + ratio * right
    along = (total_ref[...] + ridge * residual) + ratio * image_ref[...]
    points_ref[...] = alpha * right + step * direction
    left_ref[...] = residual - step * along


def call(kernel, shapes, scratch=(), flops=2_000_000, **more):
    return pl.pallas_call(
        kernel,
        out_shape=[jax.ShapeDtypeStruct(shape, f32) for shape in shapes],
        scratch_shapes=[pltpu.VMEM(shape, f32) for shape in scratch],
        compiler_params=pltpu.CompilerParams(vmem_limit_bytes=40 << 20),
        cost_estimate=pl.CostEstimate(flops=flops * 1000, bytes_accessed=1 << 20, transcendentals=0),
        **more,
    )


def body(obs_weight, magnitude, star_id, peer_count, zp_index):
    n_sky, n_exp = lax.axis_size("sky"), lax.axis_size("exp")
    cap = obs_weight.shape[3]
    tall, star, slots = (ZP_ROWS, LANES), (STAR_ROWS, LANES), (n_exp, cap)
    terms = (n_sky * n_exp, cap // LANES, LANES)
    picks = (n_exp * (cap // LANES + 1), LANES)
    vmem = pl.BlockSpec(memory_space=pltpu.VMEM)
    smem = pl.BlockSpec(memory_space=pltpu.SMEM)
    me = jnp.reshape(lax.axis_index("sky"), (1,)).astype(jnp.int32)

    def to_owners(x):
        return lax.all_to_all(x, ("sky", "exp"), split_axis=0, concat_axis=0, tiled=True)

    def to_sources(x):
        return lax.all_to_all(x, "exp", split_axis=0, concat_axis=0, tiled=True)

    zp = [zp_index] + [lax.ppermute(zp_index, "sky", [(i, i ^ d) for i in range(n_sky)]) for d in range(1, n_sky)]
    anywhere = pl.BlockSpec(memory_space=pl.ANY)
    whole = (1, 1, n_exp, cap)
    sent, live, scale = pl.pallas_call(
        functools.partial(first_terms, n_sky),
        out_shape=[jax.ShapeDtypeStruct(shape, f32) for shape in (terms, slots, star)],
        in_specs=[anywhere] * 4,
        scratch_shapes=[pltpu.SMEM((1, 1, n_exp), jnp.int32), pltpu.VMEM(whole, f32), pltpu.VMEM(whole, f32), pltpu.VMEM(whole, jnp.int32),
                        pltpu.VMEM(slots, f32), pltpu.VMEM(star, f32), pltpu.VMEM(star, f32), pltpu.SemaphoreType.DMA((4,))],
        compiler_params=pltpu.CompilerParams(vmem_limit_bytes=58 << 20),
        cost_estimate=pl.CostEstimate(flops=2_000_000_000, bytes_accessed=1 << 20, transcendentals=0),
    )(peer_count, obs_weight, magnitude, star_id)
    arrived = to_owners(sent)
    (part,) = call(own_owner, [tall], in_specs=[smem, vmem, vmem])(me, arrived, zp_index)
    sent, zp_all, right = pl.pallas_call(
        functools.partial(first_owner, n_sky),
        out_shape=[jax.ShapeDtypeStruct((n_exp * (cap // LANES), LANES), f32), jax.ShapeDtypeStruct((n_sky * n_exp, cap), jnp.int32), jax.ShapeDtypeStruct(tall, f32)],
        in_specs=[smem] + [vmem] * (n_sky + 2),
        scratch_shapes=[pltpu.VMEM((n_sky * ZP_ROWS, LANES), f32), pltpu.VMEM(tall, f32)],
        compiler_params=pltpu.CompilerParams(vmem_limit_bytes=40 << 20),
    )(me, arrived, part, *zp)
    first = to_sources(sent.reshape(n_exp, cap // LANES, LANES))
    (sent,) = call(functools.partial(second_terms, n_sky), [terms], [slots, slots, star, star])(first, star_id, live, scale)
    arrived = to_owners(sent)
    sent, image = call(second_owner, [picks, tall])(arrived, zp_all, right, zp_index)
    second = to_sources(sent.reshape(n_exp, cap + LANES))
    sent, residual, scalars = call(
        functools.partial(third_terms, n_sky), [(n_sky * n_exp * (cap // LANES + 1), LANES), tall, (SUB, LANES)], [slots, slots, star, star]
    )(first, second, star_id, live, scale, right, image)
    arrived = to_owners(sent.reshape(n_sky * n_exp, cap + LANES))
    points, left = call(last_owner, [tall, tall], [tall])(arrived, zp_all, right, image, residual, scalars)
    return points.reshape(-1)[:ZP_DEV], left.reshape(-1)[:ZP_DEV]


def solution(mesh):
    return jax.shard_map(
        body,
        mesh=mesh,
        in_specs=(
            P("sky", "exp", None, None),
            P("sky", "exp", None, None),
            P("sky", "exp", None, None),
            P("sky", "exp", None),
            P("sky", "exp", None, None),
        ),
        out_specs=(P("exp"), P("exp")),
        check_vma=False,
    )
```

```python
import functools
import math

import jax
import jax.numpy as jnp
from jax import lax
from jax.experimental import pallas as pl
from jax.experimental.pallas import tpu as pltpu
from jax.sharding import PartitionSpec as P

STAR_DEV = 4096
ZP_DEV = 12096
LANES = 128
SUB = 8
ridge = 1.0
prior = 1.0

f32 = jnp.float32
bf16 = jnp.bfloat16
i16 = jnp.int16
STAR_ROWS = STAR_DEV // LANES
ZP_ROWS = -(-ZP_DEV // (LANES * 16)) * 16
HALF_ROWS = ZP_ROWS // 2
OWNER_BLOCK = 32


def hot_rows(upper_index, lower_index, values, rows, columns):
    position = lax.broadcasted_iota(i16, (16, LANES), 0)
    high = jnp.broadcast_to(upper_index, (16, LANES)).astype(i16)
    one, zero = jnp.ones((), bf16), jnp.zeros((), bf16)
    masks = [position + jnp.int16(16 * step) == high for step in range(rows // 16)]
    upper = []
    for value in values:
        spread = jnp.broadcast_to(value, (16, LANES)).astype(bf16)
        upper.extend(jnp.where(mask, spread, zero) for mask in masks)
    low = jnp.broadcast_to(lower_index.astype(f32), (LANES, LANES)).astype(bf16).T
    lane = lax.broadcasted_iota(jnp.int32, (LANES, LANES), 1).astype(f32).astype(bf16)
    lower = [
        jnp.where(low == lane + jnp.asarray(start, bf16), one, zero)[:, :min(LANES, columns - start)]
        for start in range(0, columns, LANES)
    ]
    return jnp.concatenate(upper, 0), jnp.concatenate(lower, 1)


def halves(value):
    top = value.astype(bf16).astype(f32)
    return [top, value - top]


def sum_rows(entries, rows, columns):
    uppers, lowers = [], []
    for upper_index, lower_index, values in entries:
        parts = [part for value in values for part in halves(value)]
        upper, lower = hot_rows(upper_index, lower_index, parts, rows, columns)
        uppers.append(upper)
        lowers.append(lower)
    total = jnp.dot(jnp.concatenate(uppers, 1), jnp.concatenate(lowers, 0), preferred_element_type=f32)
    return [total[2 * n * rows:(2 * n + 1) * rows] + total[(2 * n + 1) * rows:(2 * n + 2) * rows] for n in range(len(entries[0][2]))]


def pick(table_ref, index, rows):
    high, low = index >> 7, index & 127
    found = jnp.zeros((SUB, LANES), f32)
    for row in range(rows):
        line = jnp.broadcast_to(table_ref[row:row + 1, :], (SUB, LANES))
        found = jnp.where(high == row, jnp.take_along_axis(line, low, axis=1), found)
    return found


def tiles(n_rows, cap):
    return [(g, a) for g in range(n_rows // SUB) for a in range(cap // LANES)]


def at(g, a):
    return (pl.ds(g * SUB, SUB), pl.ds(a * LANES, LANES))


def lane_row(ref, r, a):
    return ref[r:r + 1, a * LANES:(a + 1) * LANES]


def whole_sum(x):
    return jnp.sum(jnp.sum(x, axis=1, keepdims=True), axis=0, keepdims=True)


def star_sums(star_ref, value_refs, n_rows, cap, sums_refs):
    for ref in sums_refs:
        ref[...] = jnp.zeros_like(ref)

    def block(g, carry):
        stars = star_ref[pl.ds(pl.multiple_of(g * SUB, SUB), SUB), :]
        values = [ref[pl.ds(pl.multiple_of(g * SUB, SUB), SUB), :] for ref in value_refs]
        high, low = stars >> 7, stars & 127
        pairs = []
        for r in range(SUB):
            for a in range(cap // LANES):
                cut = (slice(r, r + 1), slice(a * LANES, (a + 1) * LANES))
                pairs.append((high[cut], low[cut], [value[cut] for value in values]))
        for ref, part in zip(sums_refs, sum_rows(pairs, STAR_ROWS, LANES)):
            ref[...] += part
        return carry

    lax.fori_loop(0, n_rows // SUB, block, 0)


def first_terms(n_sky, count_from, weight_from, magnitude_from, star_from, terms_ref, live_ref, scale_ref,
                count_ref, weight_ref, magnitude_ref, star_ref, moment_ref, sums_ref, mean_ref, arrival):
    n_rows, cap = weight_from.shape[2:]
    copies = [
        pltpu.make_async_copy(source, target, arrival.at[n])
        for n, (source, target) in enumerate(
            [(count_from, count_ref), (weight_from, weight_ref), (magnitude_from, magnitude_ref), (star_from, star_ref)])
    ]
    for copy in copies:
        copy.start()
    for copy in copies:
        copy.wait()
    sub = lax.broadcasted_iota(jnp.int32, (SUB, LANES), 0)
    lane = lax.broadcasted_iota(jnp.int32, (SUB, LANES), 1)
    for g in range(n_rows // SUB):
        count = jnp.zeros((SUB, LANES), jnp.int32)
        for r in range(SUB):
            count = jnp.where(sub == r, count_ref[0, 0, g * SUB + r], count)
        for a in range(cap // LANES):
            where = at(g, a)
            live = jnp.where(lane + a * LANES < count, weight_ref[(0, 0) + where], 0.0)
            live_ref[where] = live
            moment_ref[where] = live * magnitude_ref[(0, 0) + where]
    star_sums(star_ref.at[0, 0], [live_ref, moment_ref], n_rows, cap, [scale_ref, sums_ref])
    scale_ref[...] = 1.0 / (prior + scale_ref[...])
    mean_ref[...] = sums_ref[...] * scale_ref[...]
    for g in range(n_rows // SUB):
        for a in range(cap // LANES):
            where = at(g, a)
            mean = pick(mean_ref, star_ref[(0, 0) + where], STAR_ROWS)
            term = live_ref[where] * (magnitude_ref[(0, 0) + where] - mean)
            for i in range(n_sky):
                terms_ref[i * n_rows + g * SUB:i * n_rows + (g + 1) * SUB, a, :] = term


def owner_sums(zp_ref, arrived, n_rows, cap, total_ref, most=OWNER_BLOCK):
    total_ref[...] = jnp.zeros_like(total_ref)
    step = math.gcd(n_rows, most)

    def block(n, carry):
        entries = []
        for g in range(step // SUB):
            first = pl.multiple_of(n * step + g * SUB, SUB)
            index = zp_ref[pl.ds(first, SUB), :]
            row, lane = index >> 7, index & 127
            beyond = row >= HALF_ROWS
            high = jnp.where(beyond, row - HALF_ROWS, row)
            low = jnp.where(beyond, lane + LANES, lane)
            for r in range(SUB):
                for a in range(cap // LANES):
                    cut = (slice(r, r + 1), slice(a * LANES, (a + 1) * LANES))
                    entries.append((high[cut], low[cut], [arrived(first, r, a)]))
        total = sum_rows(entries, HALF_ROWS, 2 * LANES)[0]
        total_ref[0:HALF_ROWS, :] += total[:, 0:LANES]
        total_ref[HALF_ROWS:ZP_ROWS, :] += total[:, LANES:2 * LANES]
        return carry

    lax.fori_loop(0, n_rows // step, block, 0)


def send_picks(zp_ref, table_ref, out_ref, extra=0):
    n_rows, cap = zp_ref.shape[2:]
    block = cap // LANES + extra
    for g in range(n_rows // SUB):
        rows = slice(g * SUB, (g + 1) * SUB)

        def one(a, carry, rows=rows):
            lanes = pl.ds(pl.multiple_of(a * LANES, LANES), LANES)
            index = zp_ref[0, 0, rows, lanes]
            out_ref[pl.ds(rows.start * block + a, SUB, stride=block), :] = pick(table_ref, index, ZP_ROWS)
            return carry

        lax.fori_loop(0, cap // LANES, one, 0, unroll=4)


def own_owner(me_ref, arrived_ref, zp_ref, part_ref):
    n_rows, cap = zp_ref.shape[2:]
    base = me_ref[0] * n_rows

    def arrived(first, r, a):
        return arrived_ref[pl.ds(base + first + r, 1), a, :]

    owner_sums(zp_ref.at[0, 0], arrived, n_rows, cap, part_ref)


def first_owner(n_sky, me_ref, arrived_ref, part_ref, *refs):
    zp_refs, (sent_ref, all_ref, right_ref, parts_ref, one_ref) = refs[:n_sky], refs[n_sky:]
    n_rows, cap = zp_refs[0].shape[2:]
    parts_ref[pl.ds(pl.multiple_of(me_ref[0] * ZP_ROWS, SUB), ZP_ROWS), :] = part_ref[...]
    for d in range(n_sky):
        group = me_ref[0] ^ d
        base = pl.multiple_of(group * n_rows, SUB)
        all_ref[pl.ds(base, n_rows), :] = zp_refs[d][0, 0]
        if d:

            def arrived(first, r, a, base=base):
                return arrived_ref[pl.ds(base + first + r, 1), a, :]

            owner_sums(zp_refs[d].at[0, 0], arrived, n_rows, cap, one_ref)
            parts_ref[pl.ds(pl.multiple_of(group * ZP_ROWS, SUB), ZP_ROWS), :] = one_ref[...]
    right = parts_ref[0:ZP_ROWS, :]
    for n in range(1, n_sky):
        right = right + parts_ref[n * ZP_ROWS:(n + 1) * ZP_ROWS, :]
    right_ref[...] = right
    send_picks(zp_refs[0], right_ref, sent_ref)


def star_terms(n_sky, star_ref, live_ref, scale_ref, slot_ref, product_ref, sums_ref, mean_ref, emit):
    n_rows, cap = live_ref.shape
    for g, a in tiles(n_rows, cap):
        product_ref[at(g, a)] = live_ref[at(g, a)] * slot_ref[at(g, a)]
    star_sums(star_ref.at[0, 0], [product_ref], n_rows, cap, [sums_ref])
    mean_ref[...] = sums_ref[...] * scale_ref[...]
    along = jnp.zeros((SUB, LANES), f32)
    for g, a in tiles(n_rows, cap):
        where = at(g, a)
        mean = pick(mean_ref, star_ref[(0, 0) + where], STAR_ROWS)
        slot = slot_ref[where]
        term = live_ref[where] * (slot - mean)
        along = along + slot * term
        emit(g, a, term)
    return whole_sum(along)


def second_terms(n_sky, values_ref, star_ref, live_ref, scale_ref, terms_ref, slot_ref, product_ref, sums_ref, mean_ref):
    n_rows, cap = live_ref.shape
    for g, a in tiles(n_rows, cap):
        slot_ref[at(g, a)] = values_ref[g * SUB:(g + 1) * SUB, a, :]

    def emit(g, a, term):
        for i in range(n_sky):
            terms_ref[i * n_rows + g * SUB:i * n_rows + (g + 1) * SUB, a, :] = term

    star_terms(n_sky, star_ref, live_ref, scale_ref, slot_ref, product_ref, sums_ref, mean_ref, emit)


def second_owner(arrived_ref, all_ref, right_ref, zp_ref, sent_ref, image_ref):
    n_rows, cap = zp_ref.shape[2:]

    def arrived(first, r, a):
        return arrived_ref[pl.ds(first + r, 1), a, :]

    owner_sums(all_ref, arrived, all_ref.shape[0], cap, image_ref, 32)
    right = right_ref[...]
    image_ref[...] = image_ref[...] + ridge * right
    send_picks(zp_ref, image_ref, sent_ref, 1)
    lane = lax.broadcasted_iota(jnp.int32, (1, LANES), 1)
    both = jnp.where(lane < LANES // 2, whole_sum(right * right), whole_sum(right * image_ref[...]))
    block = cap // LANES + 1
    sent_ref[pl.ds(block - 1, n_rows, stride=block), :] = jnp.broadcast_to(both, (n_rows, LANES))


def third_terms(n_sky, first_ref, second_ref, star_ref, live_ref, scale_ref, right_ref, image_ref,
                terms_ref, residual_ref, scalar_ref, slot_ref, product_ref, sums_ref, mean_ref):
    n_rows, cap = live_ref.shape
    extra = cap // LANES
    sums = jnp.sum(second_ref[:, cap:cap + LANES], axis=0, keepdims=True)
    norm = jnp.broadcast_to(sums[:, 0:1], (1, LANES))
    product = jnp.broadcast_to(sums[:, LANES // 2:LANES // 2 + 1], (1, LANES))
    alpha = norm / product
    scalar_ref[0:1, :] = norm
    scalar_ref[1:2, :] = alpha
    residual = right_ref[...] - alpha * image_ref[...]
    residual_ref[...] = residual
    square = whole_sum(residual * residual)
    for g, a in tiles(n_rows, cap):
        rows = slice(g * SUB, (g + 1) * SUB)
        slot_ref[at(g, a)] = first_ref[rows, a, :] - alpha * second_ref[at(g, a)]

    def emit(g, a, term):
        for i in range(n_sky):
            terms_ref[pl.ds((i * n_rows + g * SUB) * (extra + 1) + a, SUB, stride=extra + 1), :] = term

    along = star_terms(n_sky, star_ref, live_ref, scale_ref, slot_ref, product_ref, sums_ref, mean_ref, emit)
    lane = lax.broadcasted_iota(jnp.int32, (1, LANES), 1)
    both = jnp.where(lane < LANES // 2, along, square * (1.0 / n_sky))
    terms_ref[pl.ds(extra, n_sky * n_rows, stride=extra + 1), :] = jnp.broadcast_to(both, (n_sky * n_rows, LANES))


def last_owner(arrived_ref, all_ref, right_ref, image_ref, residual_ref, scalar_ref, points_ref, left_ref, total_ref):
    cap = all_ref.shape[1]

    def arrived(first, r, a):
        return arrived_ref[pl.ds(first, SUB), a * LANES:(a + 1) * LANES][r:r + 1]

    owner_sums(all_ref, arrived, all_ref.shape[0], cap, total_ref)
    sums = jnp.sum(arrived_ref[:, cap:cap + LANES], axis=0, keepdims=True)
    norm_next = sums[:, LANES // 2:LANES // 2 + 1]
    product = sums[:, 0:1] + ridge * norm_next
    norm, alpha = scalar_ref[0:1, 0:1], scalar_ref[1:2, 0:1]
    ratio = norm_next / norm
    step = norm_next / (product - ratio * norm_next / alpha)
    right, residual = right_ref[...], residual_ref[...]
    direction = residual + ratio * right
    along = (total_ref[...] + ridge * residual) + ratio * image_ref[...]
    points_ref[...] = alpha * right + step * direction
    left_ref[...] = residual - step * along


def call(kernel, shapes, scratch=(), flops=2_000_000, **more):
    return pl.pallas_call(
        kernel,
        out_shape=[jax.ShapeDtypeStruct(shape, f32) for shape in shapes],
        scratch_shapes=[pltpu.VMEM(shape, f32) for shape in scratch],
        compiler_params=pltpu.CompilerParams(vmem_limit_bytes=40 << 20),
        cost_estimate=pl.CostEstimate(flops=flops * 1000, bytes_accessed=1 << 20, transcendentals=0),
        **more,
    )


def body(obs_weight, magnitude, star_id, peer_count, zp_index):
    n_sky, n_exp = lax.axis_size("sky"), lax.axis_size("exp")
    cap = obs_weight.shape[3]
    tall, star, slots = (ZP_ROWS, LANES), (STAR_ROWS, LANES), (n_exp, cap)
    terms = (n_sky * n_exp, cap // LANES, LANES)
    picks = (n_exp * (cap // LANES + 1), LANES)
    vmem = pl.BlockSpec(memory_space=pltpu.VMEM)
    smem = pl.BlockSpec(memory_space=pltpu.SMEM)
    me = jnp.reshape(lax.axis_index("sky"), (1,)).astype(jnp.int32)

    def to_owners(x):
        return lax.all_to_all(x, ("sky", "exp"), split_axis=0, concat_axis=0, tiled=True)

    def to_sources(x):
        return lax.all_to_all(x, "exp", split_axis=0, concat_axis=0, tiled=True)

    zp = [zp_index] + [lax.ppermute(zp_index, "sky", [(i, i ^ d) for i in range(n_sky)]) for d in range(1, n_sky)]
    anywhere = pl.BlockSpec(memory_space=pl.ANY)
    whole = (1, 1, n_exp, cap)
    sent, live, scale = pl.pallas_call(
        functools.partial(first_terms, n_sky),
        out_shape=[jax.ShapeDtypeStruct(shape, f32) for shape in (terms, slots, star)],
        in_specs=[anywhere] * 4,
        scratch_shapes=[pltpu.SMEM((1, 1, n_exp), jnp.int32), pltpu.VMEM(whole, f32), pltpu.VMEM(whole, f32), pltpu.VMEM(whole, jnp.int32),
                        pltpu.VMEM(slots, f32), pltpu.VMEM(star, f32), pltpu.VMEM(star, f32), pltpu.SemaphoreType.DMA((4,))],
        compiler_params=pltpu.CompilerParams(vmem_limit_bytes=58 << 20),
        cost_estimate=pl.CostEstimate(flops=2_000_000_000, bytes_accessed=1 << 20, transcendentals=0),
    )(peer_count, obs_weight, magnitude, star_id)
    sent, zp[1] = lax.optimization_barrier((sent, zp[1]))
    arrived = to_owners(sent)
    (part,) = call(own_owner, [tall], in_specs=[smem, vmem, vmem])(me, arrived, zp_index)
    sent, zp_all, right = pl.pallas_call(
        functools.partial(first_owner, n_sky),
        out_shape=[jax.ShapeDtypeStruct((n_exp * (cap // LANES), LANES), f32), jax.ShapeDtypeStruct((n_sky * n_exp, cap), jnp.int32), jax.ShapeDtypeStruct(tall, f32)],
        in_specs=[smem] + [vmem] * (n_sky + 2),
        scratch_shapes=[pltpu.VMEM((n_sky * ZP_ROWS, LANES), f32), pltpu.VMEM(tall, f32)],
        compiler_params=pltpu.CompilerParams(vmem_limit_bytes=40 << 20),
    )(me, arrived, part, *zp)
    first = to_sources(sent.reshape(n_exp, cap // LANES, LANES))
    (sent,) = call(functools.partial(second_terms, n_sky), [terms], [slots, slots, star, star])(first, star_id, live, scale)
    arrived = to_owners(sent)
    sent, image = call(second_owner, [picks, tall])(arrived, zp_all, right, zp_index)
    second = to_sources(sent.reshape(n_exp, cap + LANES))
    sent, residual, scalars = call(
        functools.partial(third_terms, n_sky), [(n_sky * n_exp * (cap // LANES + 1), LANES), tall, (SUB, LANES)], [slots, slots, star, star]
    )(first, second, star_id, live, scale, right, image)
    arrived = to_owners(sent.reshape(n_sky * n_exp, cap + LANES))
    points, left = call(last_owner, [tall, tall], [tall])(arrived, zp_all, right, image, residual, scalars)
    return points.reshape(-1)[:ZP_DEV], left.reshape(-1)[:ZP_DEV]


def solution(mesh):
    return jax.shard_map(
        body,
        mesh=mesh,
        in_specs=(
            P("sky", "exp", None, None),
            P("sky", "exp", None, None),
            P("sky", "exp", None, None),
            P("sky", "exp", None),
            P("sky", "exp", None, None),
        ),
        out_specs=(P("exp"), P("exp")),
        check_vma=False,
    )
```
